32 devices in a mesh: pair: 8 (over y, x, core), vir: 4 (over z).
Axes of the slice: x: 2, y: 2, z: 4, core: 2. Of those that a mesh axis runs over, the one named last changes fastest.
Arguments:
- amplitudes: bfloat16 [2048, 2048], P('pair', 'vir'), may hold values from -6 to 6
- integrals: bfloat16 [2, 512, 128, 128], P(None, ('pair', 'vir')), may hold values from -0.0625 to 0.0625
- tile_blocks: int32 [2, 512, 2], P(None, ('pair', 'vir')), may hold values from 0 to 15
- mirror_row: int32 [2048], P('pair'), may hold values from 0 to 2047, as said below
Outputs:
- symmetric: bfloat16 [2048, 2048], P('pair', 'vir')
The draws below stay inside these ranges and needn't reach their ends.
Inputs may be any that keep to these rules, and one draw needn't show every extreme that they name: mirror_row is an involution without fixed points; the mirrors of the rows of pair block k (rows k * 256 to (k + 1) * 256 - 1) all lie in block k XOR 1, in an arbitrary order.
All inputs are finite; a program needn't handle non-finite values.
Results may differ from the reference program's by a relative error of at most 0.015.
Values may be sent and summed in bfloat16 or wider, within the bound.
No kernel may reach another device: no remote copies, remote signals or barrier semaphores. Data moves between devices by JAX's collectives and lax.ppermute only.
A program may use at most 128 MiB of HBM per device.

```python
import jax
import jax.numpy as jnp
from jax import lax

TILE = 128
SUB = 8
SLABS = 2
PAIR_DEV = 256
TILE_DEV = 16
PAIRS = 2048
NBLK = 16
COLS = 2048
TILES = 512
N_PAIR = 8
N_VIR = 4


def draw_mirror_row(key, part):
    key = jax.random.fold_in(key, 11)
    couples = PAIRS // PAIR_DEV // 2
    keys = jax.random.split(key, couples)
    perms = jax.vmap(lambda sub_key: jax.random.permutation(sub_key, PAIR_DEV))(keys).astype(jnp.int32)
    inverse = jnp.argsort(perms, axis=1, stable=True).astype(jnp.int32)
    first_block = 2 * jnp.arange(couples, dtype=jnp.int32)[:, None] * PAIR_DEV
    lower = first_block + PAIR_DEV + perms
    upper = first_block + inverse
    return jnp.stack([lower, upper], axis=1).reshape(PAIRS).astype(jnp.int32)


def set_ends(values, own_key, low, top_value):
    dims = values.shape
    place = [jax.random.randint(jax.random.fold_in(own_key, axis), (), 0, dims[axis]) for axis in range(len(dims))]
    values = values.at[tuple(place)].set(low)
    longest = dims.index(max(dims))
    place[longest] = (place[longest] + 1) % dims[longest]
    return values.at[tuple(place)].set(top_value)


def shard_levels(rng, extent, cuts, low, largest):
    loudness = 1.0
    for position, shards_of in cuts:
        steps = jax.random.uniform(jax.random.fold_in(jax.random.fold_in(rng, 6), position), (shards_of,), jnp.float32, low / len(cuts), largest / len(cuts))
        loudness = loudness * jnp.repeat(jnp.exp(steps), extent[position] // shards_of).reshape((-1,) + (1,) * (len(extent) - 1 - position))
    return loudness


def centred(key, dims, scale, bound, pieces=(), held_as=jnp.bfloat16):
    drawn = jax.random.normal(key, dims, jnp.float32) * scale
    if len(pieces) > 0:
        drawn = shard_levels(key, dims, pieces, -0.22, 0.18) * drawn
    return jnp.clip(drawn, min=-bound, max=bound).astype(held_as)


def setup_inputs(seed: int = 0) -> dict:
    splits = jax.random.split(jax.random.key(seed), 5)
    return {
        "amplitudes": centred(splits[0], (PAIRS, COLS), 1.0, 6.0, ((0, 8), (1, 4))),
        "integrals": centred(splits[1], (SLABS, TILES, TILE, TILE), (TILE * max(1, SLABS * TILES // NBLK)) ** -0.5, 0.0625, ((1, 32),)),
        "tile_blocks": set_ends(jax.random.randint(splits[2], (SLABS, TILES, 2), 0, NBLK), jax.random.fold_in(splits[2], 1), 0, NBLK - 1).astype(jnp.int32),
        "mirror_row": draw_mirror_row(jax.random.fold_in(splits[4], 71), 0),
    }


def swap_virtuals(rows):
    count = rows.shape[0]
    shaped = rows.reshape(count, -1, 2, SUB, SUB)
    flipped = jnp.transpose(shaped[:, :, ::-1], (0, 1, 2, 4, 3))
    return flipped.reshape(count, -1)


def reference(amplitudes, integrals, tile_blocks, mirror_row):
    groups = SLABS * N_PAIR * N_VIR
    tile_groups = integrals.reshape(groups, TILE_DEV, TILE, TILE)
    block_groups = tile_blocks.reshape(groups, TILE_DEV, 2).astype(jnp.int32)
    column_grid = amplitudes.reshape(PAIRS, NBLK, TILE)

    def accumulate(running, item):
        tile_set, blocks = item
        picked = jnp.take(column_grid, blocks[:, 1], axis=1).astype(jnp.float32)
        products = jnp.einsum("rmc,mca->rma", picked, tile_set.astype(jnp.float32))
        return running.at[:, blocks[:, 0]].add(products), None

    running = jnp.zeros((PAIRS, NBLK, TILE), jnp.float32)
    running, _ = lax.scan(accumulate, running, (tile_groups, block_groups))
    ladder = running.reshape(PAIRS, COLS).astype(jnp.bfloat16)
    partner = jnp.take(ladder, mirror_row.astype(jnp.int32), axis=0)
    swapped = swap_virtuals(partner)
    return (ladder.astype(jnp.float32) + swapped.astype(jnp.float32)).astype(jnp.bfloat16)
```

```python
import functools

import jax
import jax.numpy as jnp
from jax import lax
from jax.experimental import pallas as pl
from jax.experimental.pallas import tpu as pltpu
from jax.sharding import PartitionSpec as P

TILE = 128
SUB = 8
F32 = jnp.float32
BF16 = jnp.bfloat16
VMEM = pl.BlockSpec(memory_space=pltpu.VMEM)
SMEM = pl.BlockSpec(memory_space=pltpu.SMEM)


def call(body, out_shape, in_specs, scratch=(), megabytes=32, flops=0, moved=0):
    many = isinstance(out_shape, (list, tuple))
    return pl.pallas_call(
        body,
        out_shape=out_shape,
        in_specs=in_specs,
        out_specs=[VMEM] * len(out_shape) if many else VMEM,
        scratch_shapes=list(scratch),
        compiler_params=pltpu.CompilerParams(vmem_limit_bytes=megabytes << 20),
        cost_estimate=pl.CostEstimate(flops=flops, bytes_accessed=moved, transcendentals=0),
    )


def swap_matrix():
    source = lax.broadcasted_iota(jnp.int32, (TILE, TILE), 0)
    target = lax.broadcasted_iota(jnp.int32, (TILE, TILE), 1)
    h, a, b = target // (SUB * SUB), target // SUB % SUB, target % SUB
    return source == (1 - h) * SUB * SUB + b * SUB + a


def order_rows_kernel(amp_ref, mirror_ref, out_ref):
    rows = amp_ref.shape[0]
    pair = lax.axis_index("pair")
    own = lax.broadcasted_iota(jnp.int32, (1, rows), 1)
    place = jnp.where(pair % 2 == 1, mirror_ref[...] - (pair - 1) * rows, own)
    hot = (lax.broadcasted_iota(jnp.int32, (rows, rows), 0) == place).astype(BF16)
    out_ref[...] = jnp.dot(hot, amp_ref[...], preferred_element_type=F32).astype(BF16)


def add_products(grid_ref, acc_ref, tiles_ref, blocks_ref):
    count = tiles_ref.shape[0]

    @pl.loop(0, count, unroll=4)
    def _(t):
        to, come = blocks_ref[2 * t], blocks_ref[2 * t + 1]
        acc_ref[to] += jnp.dot(grid_ref[come], tiles_ref[t], preferred_element_type=F32)


def fold(acc_ref, swap, block, rows):
    upper = acc_ref[block, rows:].astype(BF16)
    return acc_ref[block, :rows] + jnp.dot(upper, swap, preferred_element_type=F32)


def first_kernel(n_vir, n_sets, *refs):
    own, other = refs[:n_vir], refs[n_vir : 2 * n_vir]
    tiles = refs[2 * n_vir : 2 * n_vir + n_sets]
    blocks = refs[2 * n_vir + n_sets : 2 * n_vir + 2 * n_sets]
    grid_ref, sum_ref, acc_ref = refs[2 * n_vir + 2 * n_sets :]
    rows, width = own[0].shape
    per = width // TILE
    core = lax.axis_index("pair") % 2
    vir = lax.axis_index("vir")
    for shift in range(n_vir):
        first = (vir + n_vir - shift) % n_vir * per
        for k in range(per):
            columns = slice(k * TILE, (k + 1) * TILE)
            grid_ref[first + k, pl.ds(pl.multiple_of(core * rows, rows), rows)] = own[shift][:, columns]
            grid_ref[first + k, pl.ds(pl.multiple_of((1 - core) * rows, rows), rows)] = other[shift][:, columns]
    acc_ref[...] = jnp.zeros_like(acc_ref)
    for tiles_ref, blocks_ref in zip(tiles, blocks):
        add_products(grid_ref, acc_ref, tiles_ref, blocks_ref)
    swap = swap_matrix().astype(BF16)

    @pl.loop(0, sum_ref.shape[0])
    def _(block):
        sum_ref[block] = fold(acc_ref, swap, block, rows)


def second_kernel(n_vir, n_sets, *refs):
    grid_ref, sum_ref = refs[:2]
    tiles, blocks = refs[2 : 2 + n_sets], refs[2 + n_sets : 2 + 2 * n_sets]
    keep_ref, send_ref, acc_ref = refs[2 + 2 * n_sets :]
    rows = sum_ref.shape[1]
    half = keep_ref.shape[1]
    core = lax.axis_index("pair") % 2
    vir = lax.axis_index("vir")
    acc_ref[...] = jnp.zeros_like(acc_ref)
    for tiles_ref, blocks_ref in zip(tiles, blocks):
        add_products(grid_ref, acc_ref, tiles_ref, blocks_ref)
    swap = swap_matrix().astype(BF16)
    for shift in range(n_vir):
        first = (vir + shift) % n_vir * 2 * half
        for k in range(half):
            block = first + core * half + k
            keep_ref[shift, k] = (sum_ref[block] + fold(acc_ref, swap, block, rows)).astype(BF16)
            block = first + (1 - core) * half + k
            send_ref[shift, k] = (sum_ref[block] + fold(acc_ref, swap, block, rows)).astype(BF16)


def join_kernel(keep_ref, come_ref, *outs):
    for shift, out_ref in enumerate(outs):
        out_ref[...] = (keep_ref[shift].astype(F32) + come_ref[shift].astype(F32)).astype(BF16)


def total_kernel(*refs):
    total = refs[0][...].astype(F32)
    for ref in refs[1:-1]:
        total += ref[...].astype(F32)
    refs[-1][...] = total.astype(BF16)


def finish_kernel(own_ref, other_ref, mirror_ref, out_ref):
    half, rows, _ = own_ref.shape
    pair = lax.axis_index("pair")
    core = pair % 2
    position = lax.broadcasted_iota(jnp.int32, (rows, 1), 0)
    place = jnp.where(core == 1, mirror_ref[...] - (pair - 1) * rows, position)
    hot = (lax.broadcasted_iota(jnp.int32, (rows, rows), 1) == place).astype(BF16)
    same = lax.broadcasted_iota(jnp.int32, (TILE, TILE), 0) == lax.broadcasted_iota(jnp.int32, (TILE, TILE), 1)
    swap = jnp.where(core == 1, swap_matrix().astype(F32), same.astype(F32)).astype(BF16)
    for which in range(2):
        for k in range(half):
            values = jnp.where(core == which, own_ref[k].astype(F32), other_ref[k].astype(F32)).astype(BF16)
            values = jnp.dot(values, swap, preferred_element_type=F32).astype(BF16)
            column = (which * half + k) * TILE
            out_ref[:, column : column + TILE] = jnp.dot(hot, values, preferred_element_type=F32).astype(BF16)


def local(amplitudes, integrals, tile_blocks, mirror_row):
    rows, width = amplitudes.shape
    slabs, tile_dev = integrals.shape[:2]
    n_pair, n_vir = lax.axis_size("pair"), lax.axis_size("vir")
    per = width // TILE
    n_blk = per * n_vir

    def across(array, bits):
        return lax.ppermute(array, "pair", [(i, i ^ bits) for i in range(n_pair)])

    def along(array, shift):
        return lax.ppermute(array, "vir", [(i, (i + shift) % n_vir) for i in range(n_vir)])

    own = [integrals[s] for s in range(slabs)]
    flat_blocks = tile_blocks.reshape(slabs, -1)
    tiles = {}
    for s in range(slabs):
        tiles[1, s] = across(own[s], 2)
        tiles[2, slabs - 1 - s] = across(own[slabs - 1 - s], 4)
    for s in range(slabs):
        tiles[3, s] = across(tiles[1, s], 4) if s % 2 == 0 else across(tiles[2, s], 2)
    chips = n_pair // 2
    done = 4
    while done < chips:
        for d in range(done):
            for s in range(slabs):
                tiles[d + done, s] = across(own[s] if d == 0 else tiles[d, s], 2 * done)
        done *= 2
    blocks = {d: across(flat_blocks, 2 * d) if d else flat_blocks for d in range(chips)}

    rows_in_order = call(
        order_rows_kernel, jax.ShapeDtypeStruct((rows, width), BF16), [VMEM, VMEM], megabytes=8
    )(amplitudes, mirror_row.reshape(1, rows))
    mine = [rows_in_order] + [along(rows_in_order, shift) for shift in range(1, n_vir)]
    others = [across(piece, 1) for piece in mine]

    early = [(d, s) for d in range(3) for s in range(slabs)]
    late = [(d, s) for d in range(3, chips) for s in range(slabs)]
    for s in range(slabs):
        tiles[0, s] = own[s]
    product_flops = 2 * tile_dev * 2 * rows * TILE * TILE
    grid, partial_sum = call(
        functools.partial(first_kernel, n_vir, len(early)),
        [
            jax.ShapeDtypeStruct((n_blk, 2 * rows, TILE), BF16),
            jax.ShapeDtypeStruct((n_blk, rows, TILE), F32),
        ],
        [VMEM] * (2 * n_vir + len(early)) + [SMEM] * len(early),
        [pltpu.VMEM((n_blk, 2 * rows, TILE), F32)],
        megabytes=40,
        flops=product_flops * len(early),
        moved=8 << 20,
    )(*mine, *others, *[tiles[key] for key in early], *[blocks[d][s] for d, s in early])
    piece = jax.ShapeDtypeStruct((n_vir, per // 2, rows, TILE), BF16)
    keep, send = call(
        functools.partial(second_kernel, n_vir, len(late)),
        [piece, piece],
        [VMEM] * (2 + len(late)) + [SMEM] * len(late),
        [pltpu.VMEM((n_blk, 2 * rows, TILE), F32)],
        megabytes=40,
        flops=product_flops * len(late),
        moved=6 << 20,
    )(grid, partial_sum, *[tiles[key] for key in late], *[blocks[d][s] for d, s in late])
    one = jax.ShapeDtypeStruct((per // 2, rows, TILE), BF16)
    parts = call(join_kernel, [one] * n_vir, [VMEM, VMEM], megabytes=8)(keep, across(send, 1))
    arrived = [parts[0]] + [along(parts[shift], shift) for shift in range(1, n_vir)]
    total = call(total_kernel, one, [VMEM] * n_vir, megabytes=8)(*arrived)
    return call(
        finish_kernel, jax.ShapeDtypeStruct((rows, width), BF16), [VMEM] * 3, megabytes=8
    )(total, across(total, 1), mirror_row.reshape(rows, 1))


def solution(mesh):
    in_specs = (
        P("pair", "vir"),
        P(None, ("pair", "vir"), None, None),
        P(None, ("pair", "vir"), None),
        P("pair"),
    )
    out_specs = P("pair", "vir")
    return jax.shard_map(local, mesh=mesh, in_specs=in_specs, out_specs=out_specs, check_vma=False)
```

```python
import functools

import jax
import jax.numpy as jnp
from jax import lax
from jax.experimental import pallas as pl
from jax.experimental.pallas import tpu as pltpu
from jax.sharding import PartitionSpec as P

TILE = 128
SUB = 8
F32 = jnp.float32
BF16 = jnp.bfloat16
VMEM = pl.BlockSpec(memory_space=pltpu.VMEM)
SMEM = pl.BlockSpec(memory_space=pltpu.SMEM)


def call(body, out_shape, in_specs, scratch=(), megabytes=32, flops=0, moved=0):
    many = isinstance(out_shape, (list, tuple))
    return pl.pallas_call(
        body,
        out_shape=out_shape,
        in_specs=in_specs,
        out_specs=[VMEM] * len(out_shape) if many else VMEM,
        scratch_shapes=list(scratch),
        compiler_params=pltpu.CompilerParams(vmem_limit_bytes=megabytes << 20),
        cost_estimate=pl.CostEstimate(flops=flops, bytes_accessed=moved, transcendentals=0),
    )


def iota(shape, dimension):
    return lax.broadcasted_iota(jnp.int32, shape, dimension)


def swap_matrix():
    target = iota((TILE, TILE), 1)
    h, a, b = target // (SUB * SUB), target // SUB % SUB, target % SUB
    return iota((TILE, TILE), 0) == (1 - h) * SUB * SUB + b * SUB + a


def swap_columns(tiles_ref, swapped_ref):
    swap = swap_matrix().astype(BF16)

    @pl.loop(0, tiles_ref.shape[0], unroll=4)
    def _(t):
        swapped_ref[t] = jnp.dot(tiles_ref[t], swap, preferred_element_type=F32).astype(BF16)


def swap_kernel(*refs):
    count = len(refs) // 2
    for tiles_ref, swapped_ref in zip(refs[:count], refs[count:]):
        swap_columns(tiles_ref, swapped_ref)


def add_products(grid_ref, acc_ref, tiles_ref, swapped_ref, blocks_ref, first):
    @pl.loop(0, tiles_ref.shape[0], unroll=4)
    def _(t):
        to, come = blocks_ref[2 * (first + t)], blocks_ref[2 * (first + t) + 1]
        both = jnp.concatenate([tiles_ref[t], swapped_ref[t]], axis=0)
        acc_ref[to] += jnp.dot(grid_ref[come], both, preferred_element_type=F32)


def first_kernel(n_vir, n_sets, *refs):
    own, other = refs[:n_vir], refs[n_vir : 2 * n_vir]
    tiles = refs[2 * n_vir : 2 * n_vir + n_sets]
    swapped = refs[2 * n_vir + n_sets : 2 * n_vir + 2 * n_sets]
    blocks_ref, row_ref, column_ref, grid_ref, sum_ref = refs[2 * n_vir + 2 * n_sets :]
    rows, width = own[0].shape
    per = width // TILE
    pair = lax.axis_index("pair")
    vir = lax.axis_index("vir")
    upper = pair % 2 == 1
    base = (pair ^ 1) * rows
    wanted = jnp.where(upper, row_ref[...] - base - iota((rows, rows), 0), column_ref[...] - base - iota((rows, rows), 1))
    hot = jnp.where(wanted == 0, 1.0, 0.0).astype(BF16)
    for shift in range(n_vir):
        first = (vir ^ shift) * per
        for k in range(per):
            columns = slice(k * TILE, (k + 1) * TILE)
            mine, others = own[shift][:, columns], other[shift][:, columns]
            grid_ref[first + k, :, :TILE] = jnp.where(upper, others, mine)
            moved = jnp.dot(hot, jnp.where(upper, mine, others), preferred_element_type=F32)
            grid_ref[first + k, :, TILE:] = moved.astype(BF16)
    sum_ref[...] = jnp.zeros_like(sum_ref)
    for which in range(n_sets):
        first = which * tiles[which].shape[0]
        add_products(grid_ref, sum_ref, tiles[which], swapped[which], blocks_ref, first)


def second_kernel(n_vir, n_sets, first, *refs):
    grid_ref, sum_ref, blocks_ref = refs[:3]
    tiles = refs[3 : 3 + n_sets]
    keep_ref, send_ref, acc_ref, swapped_ref = refs[3 + n_sets :]
    half = keep_ref.shape[1]
    core = lax.axis_index("pair") % 2
    vir = lax.axis_index("vir")
    acc_ref[...] = sum_ref[...]
    for which, tiles_ref in enumerate(tiles):
        swap_columns(tiles_ref, swapped_ref)
        add_products(grid_ref, acc_ref, tiles_ref, swapped_ref, blocks_ref, first + which * tiles_ref.shape[0])
    for shift in range(n_vir):
        block = (vir ^ shift) * 2 * half
        for k in range(half):
            keep_ref[shift, k] = acc_ref[block + core * half + k].astype(BF16)
            send_ref[shift, k] = acc_ref[block + (1 - core) * half + k].astype(BF16)


def join_kernel(keep_ref, come_ref, *outs):
    for shift, out_ref in enumerate(outs):
        out_ref[...] = (keep_ref[shift].astype(F32) + come_ref[shift].astype(F32)).astype(BF16)


def total_kernel(*refs):
    total = refs[0][...].astype(F32)
    for ref in refs[1:-1]:
        total += ref[...].astype(F32)
    refs[-1][...] = total.astype(BF16)


def finish_kernel(own_ref, other_ref, column_ref, out_ref):
    half, rows, _ = own_ref.shape
    pair = lax.axis_index("pair")
    upper = pair % 2 == 1
    place = jnp.where(upper, column_ref[...] - (pair ^ 1) * rows, iota((rows, 1), 0))
    hot = (iota((rows, rows), 1) == place).astype(BF16)
    same = (iota((TILE, TILE), 0) == iota((TILE, TILE), 1)).astype(F32)
    swap = jnp.where(upper, swap_matrix().astype(F32), same).astype(BF16)
    for which in range(2):
        for k in range(half):
            values = jnp.where(upper == (which == 1), own_ref[k], other_ref[k])
            values = jnp.dot(values, swap, preferred_element_type=F32).astype(BF16)
            column = (which * half + k) * TILE
            out_ref[:, column : column + TILE] = jnp.dot(hot, values, preferred_element_type=F32).astype(BF16)


def local(amplitudes, integrals, tile_blocks, mirror_row):
    rows, width = amplitudes.shape
    slabs, tile_dev = integrals.shape[:2]
    n_pair, n_vir = lax.axis_size("pair"), lax.axis_size("vir")
    chips = n_pair // 2
    per = width // TILE
    n_blk = per * n_vir
    count = slabs * tile_dev

    def across(array, bits):
        return lax.ppermute(array, "pair", [(i, i ^ bits) for i in range(n_pair)])

    def along(array, bits):
        return lax.ppermute(array, "vir", [(i, i ^ bits) for i in range(n_vir)])

    tiles_x, tiles_y = across(integrals, 2), across(integrals, 4)
    shifts = list(range(n_vir // 2, n_vir)) + list(range(1, n_vir // 2))
    pieces = {shift: along(amplitudes, shift) for shift in shifts}
    pieces[0] = amplitudes
    late = [across(tiles_x[s], 4) if s % 2 == 0 else across(tiles_y[s], 2) for s in range(slabs)]

    blocks, _ = lax.optimization_barrier((tile_blocks.reshape(-1), pieces[1]))
    reach = 1
    while reach < chips:
        blocks = jnp.concatenate([blocks, across(blocks, 2 * reach)])
        reach *= 2
    reach = 4
    farther = [integrals, tiles_x, tiles_y, jnp.stack(late)] if reach < chips else []
    while reach < chips:
        farther += [across(array, 2 * reach) for array in farther]
        reach *= 2
    late += [array[s] for array in farther[4:] for s in range(slabs)]

    mine = [pieces[shift] for shift in range(n_vir)]
    others = [across(piece, 1) for piece in mine]
    row, column = mirror_row.reshape(1, rows), mirror_row.reshape(rows, 1)

    early = [array.reshape(count, TILE, TILE) for array in (integrals, tiles_x, tiles_y)]
    swapped = call(
        swap_kernel,
        [jax.ShapeDtypeStruct((count, TILE, TILE), BF16)] * len(early),
        [VMEM] * len(early),
        megabytes=16,
    )(*early)
    grid, partial_sum = call(
        functools.partial(first_kernel, n_vir, len(early)),
        [
            jax.ShapeDtypeStruct((n_blk, rows, 2 * TILE), BF16),
            jax.ShapeDtypeStruct((n_blk, rows, TILE), F32),
        ],
        [VMEM] * (2 * n_vir + 2 * len(early)) + [SMEM, VMEM, VMEM],
        megabytes=32,
    )(*mine, *others, *early, *swapped, blocks, row, column)
    piece = jax.ShapeDtypeStruct((n_vir, per // 2, rows, TILE), BF16)
    keep, send = call(
        functools.partial(second_kernel, n_vir, len(late), len(early) * count),
        [piece, piece],
        [VMEM, VMEM, SMEM] + [VMEM] * len(late),
        [pltpu.VMEM((n_blk, rows, TILE), F32), pltpu.VMEM((tile_dev, TILE, TILE), BF16)],
        megabytes=32,
    )(grid, partial_sum, blocks, *late)
    one = jax.ShapeDtypeStruct((per // 2, rows, TILE), BF16)
    parts = call(join_kernel, [one] * n_vir, [VMEM, VMEM], megabytes=8)(keep, across(send, 1))
    arrived = [along(parts[shift], shift) for shift in shifts]
    total = call(total_kernel, one, [VMEM] * n_vir, megabytes=8)(parts[0], *arrived)
    return call(
        finish_kernel, jax.ShapeDtypeStruct((rows, width), BF16), [VMEM] * 3, megabytes=8
    )(total, across(total, 1), column)


def solution(mesh):
    in_specs = (
        P("pair", "vir"),
        P(None, ("pair", "vir"), None, None),
        P(None, ("pair", "vir"), None),
        P("pair"),
    )
    out_specs = P("pair", "vir")
    return jax.shard_map(local, mesh=mesh, in_specs=in_specs, out_specs=out_specs, check_vma=False)
```

```python
import functools

import jax
import jax.numpy as jnp
from jax import lax
from jax.experimental import pallas as pl
from jax.experimental.pallas import tpu as pltpu
from jax.sharding import PartitionSpec as P

TILE = 128
SUB = 8
EXTRA = 16
F32 = jnp.float32
BF16 = jnp.bfloat16
VMEM = pl.BlockSpec(memory_space=pltpu.VMEM)
SMEM = pl.BlockSpec(memory_space=pltpu.SMEM)


def call(body, out_shape, in_specs, scratch=(), megabytes=32, aliases=None):
    many = isinstance(out_shape, (list, tuple))
    return pl.pallas_call(
        body,
        out_shape=out_shape,
        in_specs=in_specs,
        out_specs=[VMEM] * len(out_shape) if many else VMEM,
        scratch_shapes=list(scratch),
        compiler_params=pltpu.CompilerParams(vmem_limit_bytes=megabytes << 20),
        input_output_aliases=aliases or {},
        cost_estimate=pl.CostEstimate(flops=0, bytes_accessed=0, transcendentals=0),
    )


def iota(shape, dimension):
    return lax.broadcasted_iota(jnp.int32, shape, dimension)


def swap_matrix():
    target = iota((TILE, TILE), 1)
    h, a, b = target // (SUB * SUB), target // SUB % SUB, target % SUB
    return iota((TILE, TILE), 0) == (1 - h) * SUB * SUB + b * SUB + a


def pack_kernel(integrals_ref, blocks_ref, *refs):
    outs, sems = refs[:-1], refs[-1]
    length = integrals_ref.shape[1]
    copies = [
        pltpu.make_async_copy(integrals_ref.at[s], out_ref.at[pl.ds(0, length)], sems.at[s])
        for s, out_ref in enumerate(outs)
    ]
    for copy in copies:
        copy.start()
    lane = iota((EXTRA, TILE), 1)
    for s, out_ref in enumerate(outs):
        ids = jnp.zeros((EXTRA, TILE), jnp.int32)
        for t in range(length // TILE):
            for which in range(2):
                ids = jnp.where(lane == 2 * t + which, blocks_ref[s, which, t], ids)
        out_ref[length:, :] = ids.astype(F32).astype(BF16)
    for copy in copies:
        copy.wait()


def add_products(grid_ref, acc_refs, tiles_ref, blocks_ref):
    empty = jnp.zeros((TILE, TILE), BF16)

    @pl.loop(0, blocks_ref.shape[0] // 4, unroll=4)
    def _(t):
        to = [blocks_ref[4 * t + 2 * k] for k in range(2)]
        come = [blocks_ref[4 * t + 2 * k + 1] for k in range(2)]
        tiles = [tiles_ref[pl.ds(pl.multiple_of((2 * t + k) * TILE, TILE), TILE), :] for k in range(2)]
        left = jnp.concatenate([grid_ref[come[0]], grid_ref[come[1]]], axis=1)
        right = jnp.concatenate(
            [jnp.concatenate([tiles[0], empty], axis=1), jnp.concatenate([empty, tiles[1]], axis=1)], axis=0
        )
        products = jnp.dot(left, right, preferred_element_type=F32)
        for k in range(2):
            acc_refs[k][to[k]] += products[:, k * TILE : (k + 1) * TILE]


def first_kernel(n_vir, n_sets, *refs):
    own, other = refs[:n_vir], refs[n_vir : 2 * n_vir]
    tiles = refs[2 * n_vir : 2 * n_vir + n_sets]
    blocks = refs[2 * n_vir + n_sets : 2 * n_vir + 2 * n_sets]
    row_ref, column_ref, grid_ref, *acc_refs = refs[2 * n_vir + 2 * n_sets :]
    rows, width = own[0].shape
    per = width // TILE
    pair = lax.axis_index("pair")
    vir = lax.axis_index("vir")
    upper = pair % 2 == 1
    base = (pair ^ 1) * rows
    wanted = jnp.where(upper, row_ref[...] - base - iota((rows, rows), 0), column_ref[...] - base - iota((rows, rows), 1))
    hot = jnp.where(wanted == 0, 1.0, 0.0).astype(BF16)
    for shift in range(n_vir):
        first = (vir ^ shift) * per
        mine, others = own[shift][...], other[shift][...]
        kept = jnp.where(upper, others, mine)
        moved = jnp.dot(hot, jnp.where(upper, mine, others), preferred_element_type=F32).astype(BF16)
        for k in range(per):
            columns = slice(k * TILE, (k + 1) * TILE)
            grid_ref[first + k, :rows] = kept[:, columns]
            grid_ref[first + k, rows:] = moved[:, columns]
    for acc_ref in acc_refs:
        acc_ref[...] = jnp.zeros_like(acc_ref)
    for tiles_ref, blocks_ref in zip(tiles, blocks):
        add_products(grid_ref, acc_refs, tiles_ref, blocks_ref)


def second_kernel(n_vir, n_sets, *refs):
    grid_ref = refs[0]
    tiles, blocks = refs[3 : 3 + n_sets], refs[3 + n_sets : 3 + 2 * n_sets]
    keep_ref, send_ref, *acc_refs = refs[3 + 2 * n_sets :]
    half, rows = keep_ref.shape[1:3]
    core = lax.axis_index("pair") % 2
    vir = lax.axis_index("vir")
    for tiles_ref, blocks_ref in zip(tiles, blocks):
        add_products(grid_ref, acc_refs, tiles_ref, blocks_ref)
    swap = swap_matrix().astype(BF16)
    for shift in range(n_vir):
        for k in range(half):
            for out_ref, side in ((keep_ref, core), (send_ref, 1 - core)):
                block = ((vir ^ shift) * 2 + side) * half + k
                lower = acc_refs[0][block, :rows] + acc_refs[1][block, :rows]
                upper = (acc_refs[0][block, rows:] + acc_refs[1][block, rows:]).astype(BF16)
                out_ref[shift, k] = (lower + jnp.dot(upper, swap, preferred_element_type=F32)).astype(BF16)


def join_kernel(keep_ref, come_ref, *outs):
    for shift, out_ref in enumerate(outs):
        out_ref[...] = (keep_ref[shift].astype(F32) + come_ref[shift].astype(F32)).astype(BF16)


def total_kernel(*refs):
    total = refs[0][...].astype(F32)
    for ref in refs[1:-1]:
        total += ref[...].astype(F32)
    refs[-1][...] = total.astype(BF16)


def finish_kernel(own_ref, other_ref, column_ref, out_ref):
    half, rows, _ = own_ref.shape
    pair = lax.axis_index("pair")
    upper = pair % 2 == 1
    place = jnp.where(upper, column_ref[...] - (pair ^ 1) * rows, iota((rows, 1), 0))
    hot = (iota((rows, rows), 1) == place).astype(BF16)
    same = (iota((TILE, TILE), 0) == iota((TILE, TILE), 1)).astype(F32)
    swap = jnp.where(upper, swap_matrix().astype(F32), same).astype(BF16)
    for which in range(2):
        for k in range(half):
            values = jnp.where(upper == (which == 1), own_ref[k], other_ref[k])
            values = jnp.dot(values, swap, preferred_element_type=F32).astype(BF16)
            column = (which * half + k) * TILE
            out_ref[:, column : column + TILE] = jnp.dot(hot, values, preferred_element_type=F32).astype(BF16)


def local(amplitudes, integrals, tile_blocks, mirror_row):
    rows, width = amplitudes.shape
    slabs, tile_dev = integrals.shape[:2]
    n_pair, n_vir = lax.axis_size("pair"), lax.axis_size("vir")
    chips = n_pair // 2
    per = width // TILE
    n_blk = per * n_vir
    length = tile_dev * TILE

    def across(array, bits):
        return lax.ppermute(array, "pair", [(i, i ^ bits) for i in range(n_pair)])

    def along(array, bits):
        return lax.ppermute(array, "vir", [(i, i ^ bits) for i in range(n_vir)])

    packed = call(
        pack_kernel,
        [jax.ShapeDtypeStruct((length + EXTRA, TILE), BF16)] * slabs,
        [pl.BlockSpec(memory_space=pl.ANY), SMEM],
        [pltpu.SemaphoreType.DMA((slabs,))],
        megabytes=8,
    )(integrals.reshape(slabs, length, TILE), tile_blocks.transpose(0, 2, 1))
    tiles = {(0, s): packed[s] for s in range(slabs)}
    for s in range(slabs):
        tiles[1, s] = across(packed[s], 2)
        tiles[2, slabs - 1 - s] = across(packed[slabs - 1 - s], 4)
    for s in range(slabs):
        tiles[3, s] = across(tiles[1, s], 4) if s % 2 == 0 else across(tiles[2, s], 2)
    reach = 4
    while reach < chips:
        tiles |= {(d + reach, s): across(tiles[d, s], 2 * reach) for d in range(reach) for s in range(slabs)}
        reach *= 2

    pieces = {0: amplitudes}
    reach = 1
    while reach < n_vir:
        pieces |= {shift + reach: along(pieces[shift], reach) for shift in range(reach)}
        reach *= 2
    mine = [pieces[shift] for shift in range(n_vir)]
    others = [across(piece, 1) for piece in mine]
    row, column = mirror_row.reshape(1, rows), mirror_row.reshape(rows, 1)

    def ids(key):
        return tiles[key][length, : 2 * tile_dev].astype(jnp.int32)

    early = [(d, s) for d in range(3) for s in range(slabs)]
    late = [(d, s) for d in range(3, chips) for s in range(slabs)]
    sums = jax.ShapeDtypeStruct((n_blk, 2 * rows, TILE), F32)
    grid, *sums_so_far = call(
        functools.partial(first_kernel, n_vir, len(early)),
        [jax.ShapeDtypeStruct((n_blk, 2 * rows, TILE), BF16), sums, sums],
        [VMEM] * (2 * n_vir + len(early)) + [SMEM] * len(early) + [VMEM, VMEM],
        megabytes=32,
    )(*mine, *others, *[tiles[key] for key in early], *[ids(key) for key in early], row, column)
    piece = jax.ShapeDtypeStruct((n_vir, per // 2, rows, TILE), BF16)
    keep, send, *_ = call(
        functools.partial(second_kernel, n_vir, len(late)),
        [piece, piece, sums, sums],
        [VMEM] * (3 + len(late)) + [SMEM] * len(late),
        megabytes=32,
        aliases={1: 2, 2: 3},
    )(grid, *sums_so_far, *[tiles[key] for key in late], *[ids(key) for key in late])
    one = jax.ShapeDtypeStruct((per // 2, rows, TILE), BF16)
    parts = call(join_kernel, [one] * n_vir, [VMEM, VMEM], megabytes=8)(keep, across(send, 1))
    arrived = [along(parts[shift], shift) for shift in range(n_vir - 1, 0, -1)]
    total = call(total_kernel, one, [VMEM] * n_vir, megabytes=8)(parts[0], *arrived)
    return call(
        finish_kernel, jax.ShapeDtypeStruct((rows, width), BF16), [VMEM] * 3, megabytes=8
    )(total, across(total, 1), column)


def solution(mesh):
    in_specs = (
        P("pair", "vir"),
        P(None, ("pair", "vir"), None, None),
        P(None, ("pair", "vir"), None),
        P("pair"),
    )
    out_specs = P("pair", "vir")
    return jax.shard_map(local, mesh=mesh, in_specs=in_specs, out_specs=out_specs, check_vma=False)
```

```python
import functools

import jax
import jax.numpy as jnp
from jax import lax
from jax.experimental import pallas as pl
from jax.experimental.pallas import tpu as pltpu
from jax.sharding import PartitionSpec as P

TILE = 128
SUB = 8
EXTRA = 16
F32 = jnp.float32
BF16 = jnp.bfloat16
VMEM = pl.BlockSpec(memory_space=pltpu.VMEM)
SMEM = pl.BlockSpec(memory_space=pltpu.SMEM)


def call(body, out_shape, in_specs, scratch=(), megabytes=32, aliases=None, out_specs=None):
    many = isinstance(out_shape, (list, tuple))
    return pl.pallas_call(
        body,
        out_shape=out_shape,
        in_specs=in_specs,
        out_specs=out_specs or ([VMEM] * len(out_shape) if many else VMEM),
        scratch_shapes=list(scratch),
        compiler_params=pltpu.CompilerParams(vmem_limit_bytes=megabytes << 20),
        input_output_aliases=aliases or {},
        cost_estimate=pl.CostEstimate(flops=0, bytes_accessed=0, transcendentals=0),
    )


def iota(shape, dimension):
    return lax.broadcasted_iota(jnp.int32, shape, dimension)


def swap_matrix():
    target = iota((TILE, TILE), 1)
    h, a, b = target // (SUB * SUB), target // SUB % SUB, target % SUB
    return iota((TILE, TILE), 0) == (1 - h) * SUB * SUB + b * SUB + a


def pack_kernel(integrals_ref, blocks_ref, out_ref, ids_ref, sems):
    slabs, length = integrals_ref.shape[:2]
    copies = [
        pltpu.make_async_copy(integrals_ref.at[s], out_ref.at[s, pl.ds(0, length)], sems.at[s]) for s in range(slabs)
    ]
    for copy in copies:
        copy.start()
    lane = iota((EXTRA, TILE), 1)
    for s in range(slabs):
        ids = jnp.zeros((EXTRA, TILE), jnp.int32)
        for t in range(length // TILE):
            for which in range(2):
                ids = jnp.where(lane == 2 * t + which, blocks_ref[s, which, t], ids)
        ids_ref[s] = ids.astype(F32).astype(BF16)
        copies.append(
            pltpu.make_async_copy(ids_ref.at[s], out_ref.at[s, pl.ds(length, EXTRA)], sems.at[slabs + s])
        )
        copies[-1].start()
    for copy in copies:
        copy.wait()


def cut_kernel(x_ref, y_ref, *outs):
    for s, out_ref in enumerate(outs):
        out_ref[...] = (x_ref if s % 2 == 0 else y_ref)[s]


def add_products(grid_ref, acc_refs, tiles_ref, blocks_ref):
    empty = jnp.zeros((TILE, TILE), BF16)

    @pl.loop(0, blocks_ref.shape[0] // 4, unroll=4)
    def _(t):
        to = [blocks_ref[4 * t + 2 * k] for k in range(2)]
        come = [blocks_ref[4 * t + 2 * k + 1] for k in range(2)]
        tiles = [tiles_ref[pl.ds(pl.multiple_of((2 * t + k) * TILE, TILE), TILE), :] for k in range(2)]
        left = jnp.concatenate([grid_ref[come[0]], grid_ref[come[1]]], axis=1)
        right = jnp.concatenate(
            [jnp.concatenate([tiles[0], empty], axis=1), jnp.concatenate([empty, tiles[1]], axis=1)], axis=0
        )
        products = jnp.dot(left, right, preferred_element_type=F32)
        for k in range(2):
            acc_refs[k][to[k]] += products[:, k * TILE : (k + 1) * TILE]


def first_kernel(n_vir, n_sets, *refs):
    own, other = refs[:n_vir], refs[n_vir : 2 * n_vir]
    tiles = refs[2 * n_vir : 2 * n_vir + n_sets]
    blocks = refs[2 * n_vir + n_sets : 2 * n_vir + 2 * n_sets]
    row_ref, column_ref, grid_ref, *acc_refs = refs[2 * n_vir + 2 * n_sets :]
    rows, width = own[0].shape
    per = width // TILE
    pair = lax.axis_index("pair")
    vir = lax.axis_index("vir")
    upper = pair % 2 == 1
    base = (pair ^ 1) * rows
    wanted = jnp.where(upper, row_ref[...] - base - iota((rows, rows), 0), column_ref[...] - base - iota((rows, rows), 1))
    hot = jnp.where(wanted == 0, 1.0, 0.0).astype(BF16)
    for shift in range(n_vir):
        first = (vir ^ shift) * per
        mine, others = own[shift][...], other[shift][...]
        kept = jnp.where(upper, others, mine)
        moved = jnp.dot(hot, jnp.where(upper, mine, others), preferred_element_type=F32).astype(BF16)
        for k in range(per):
            columns = slice(k * TILE, (k + 1) * TILE)
            grid_ref[first + k, :rows] = kept[:, columns]
            grid_ref[first + k, rows:] = moved[:, columns]
    for acc_ref in acc_refs:
        acc_ref[...] = jnp.zeros_like(acc_ref)
    for tiles_ref, blocks_ref in zip(tiles, blocks):
        for s in range(tiles_ref.shape[0]):
            add_products(grid_ref, acc_refs, tiles_ref.at[s], blocks_ref.at[s])


def second_kernel(n_vir, n_sets, *refs):
    grid_ref = refs[0]
    tiles, blocks = refs[3 : 3 + n_sets], refs[3 + n_sets : 3 + 2 * n_sets]
    keep_ref, send_ref, *acc_refs = refs[3 + 2 * n_sets :]
    half, rows = keep_ref.shape[1:3]
    core = lax.axis_index("pair") % 2
    vir = lax.axis_index("vir")
    for tiles_ref, blocks_ref in zip(tiles, blocks):
        for s in range(tiles_ref.shape[0]):
            add_products(grid_ref, acc_refs, tiles_ref.at[s], blocks_ref.at[s])
    swap = swap_matrix().astype(BF16)
    for shift in range(n_vir):
        for k in range(half):
            for out_ref, side in ((keep_ref, core), (send_ref, 1 - core)):
                block = ((vir ^ shift) * 2 + side) * half + k
                lower = acc_refs[0][block, :rows] + acc_refs[1][block, :rows]
                upper = (acc_refs[0][block, rows:] + acc_refs[1][block, rows:]).astype(BF16)
                out_ref[shift, k] = (lower + jnp.dot(upper, swap, preferred_element_type=F32)).astype(BF16)


def join_kernel(keep_ref, come_ref, *outs):
    for shift, out_ref in enumerate(outs):
        out_ref[...] = (keep_ref[shift].astype(F32) + come_ref[shift].astype(F32)).astype(BF16)


def total_kernel(*refs):
    total = refs[0][...].astype(F32)
    for ref in refs[1:-1]:
        total += ref[...].astype(F32)
    refs[-1][...] = total.astype(BF16)


def finish_kernel(own_ref, other_ref, column_ref, out_ref):
    half, rows, _ = own_ref.shape
    pair = lax.axis_index("pair")
    upper = pair % 2 == 1
    place = jnp.where(upper, column_ref[...] - (pair ^ 1) * rows, iota((rows, 1), 0))
    hot = (iota((rows, rows), 1) == place).astype(BF16)
    same = (iota((TILE, TILE), 0) == iota((TILE, TILE), 1)).astype(F32)
    swap = jnp.where(upper, swap_matrix().astype(F32), same).astype(BF16)
    for which in range(2):
        for k in range(half):
            values = jnp.where(upper == (which == 1), own_ref[k], other_ref[k])
            values = jnp.dot(values, swap, preferred_element_type=F32).astype(BF16)
            column = (which * half + k) * TILE
            out_ref[:, column : column + TILE] = jnp.dot(hot, values, preferred_element_type=F32).astype(BF16)


def local(amplitudes, integrals, tile_blocks, mirror_row):
    rows, width = amplitudes.shape
    slabs, tile_dev = integrals.shape[:2]
    n_pair, n_vir = lax.axis_size("pair"), lax.axis_size("vir")
    chips = n_pair // 2
    per = width // TILE
    n_blk = per * n_vir
    length = tile_dev * TILE

    def across(array, bits):
        return lax.ppermute(array, "pair", [(i, i ^ bits) for i in range(n_pair)])

    def along(array, bits):
        return lax.ppermute(array, "vir", [(i, i ^ bits) for i in range(n_vir)])

    packed = call(
        pack_kernel,
        jax.ShapeDtypeStruct((slabs, length + EXTRA, TILE), BF16),
        [pl.BlockSpec(memory_space=pl.ANY), SMEM],
        [pltpu.VMEM((slabs, EXTRA, TILE), BF16), pltpu.SemaphoreType.DMA((2 * slabs,))],
        out_specs=pl.BlockSpec(memory_space=pl.ANY),
        megabytes=56,
    )(integrals.reshape(slabs, length, TILE), tile_blocks.transpose(0, 2, 1))
    early = [packed, across(packed, 2), across(packed, 4)]

    pieces = {0: amplitudes}
    reach = 1
    while reach < n_vir:
        pieces |= {shift + reach: along(pieces[shift], reach) for shift in range(reach)}
        reach *= 2
    mine = [pieces[shift] for shift in range(n_vir)]
    others = [across(piece, 1) for piece in mine]
    tiles_x, tiles_y, *_ = lax.optimization_barrier((*early[1:], *others[:2], *mine[:-1]))
    slab = jax.ShapeDtypeStruct((length + EXTRA, TILE), BF16)
    halves = call(cut_kernel, [slab] * slabs, [VMEM, VMEM], megabytes=8)(tiles_x, tiles_y)
    late = [across(half, 4 if s % 2 == 0 else 2) for s, half in enumerate(halves)]
    reach = 4
    while reach < chips:
        farther = early + late if reach == 4 else late
        late = late + [across(array, 2 * reach) for array in farther]
        reach *= 2
    late = [array.reshape(-1, length + EXTRA, TILE) for array in late]
    row, column = mirror_row.reshape(1, rows), mirror_row.reshape(rows, 1)

    def ids(array):
        return array[:, length, : 2 * tile_dev].astype(jnp.int32)

    sums = jax.ShapeDtypeStruct((n_blk, 2 * rows, TILE), F32)
    grid, *sums_so_far = call(
        functools.partial(first_kernel, n_vir, len(early)),
        [jax.ShapeDtypeStruct((n_blk, 2 * rows, TILE), BF16), sums, sums],
        [VMEM] * (2 * n_vir + len(early)) + [SMEM] * len(early) + [VMEM, VMEM],
        megabytes=32,
    )(*mine, *others, *early, *[ids(array) for array in early], row, column)
    piece = jax.ShapeDtypeStruct((n_vir, per // 2, rows, TILE), BF16)
    keep, send, *_ = call(
        functools.partial(second_kernel, n_vir, len(late)),
        [piece, piece, sums, sums],
        [VMEM] * (3 + len(late)) + [SMEM] * len(late),
        megabytes=32,
        aliases={1: 2, 2: 3},
    )(grid, *sums_so_far, *late, *[ids(array) for array in late])
    one = jax.ShapeDtypeStruct((per // 2, rows, TILE), BF16)
    parts = call(join_kernel, [one] * n_vir, [VMEM, VMEM], megabytes=8)(keep, across(send, 1))
    parts = dict(enumerate(parts))
    reach = 1
    while reach < n_vir:
        sent = [shift for shift in reversed(parts) if shift & reach]
        arrived = {shift: along(parts.pop(shift), reach) for shift in sent}
        for shift in sent:
            kept = shift ^ reach
            if 2 * reach < n_vir:
                parts[kept] = call(total_kernel, one, [VMEM] * 2, megabytes=8)(parts[kept], arrived[shift])
        reach *= 2
    total = call(total_kernel, one, [VMEM] * 2, megabytes=8)(parts[0], *arrived.values())
    return call(
        finish_kernel, jax.ShapeDtypeStruct((rows, width), BF16), [VMEM] * 3, megabytes=8
    )(total, across(total, 1), column)


def solution(mesh):
    in_specs = (
        P("pair", "vir"),
        P(None, ("pair", "vir"), None, None),
        P(None, ("pair", "vir"), None),
        P("pair"),
    )
    out_specs = P("pair", "vir")
    return jax.shard_map(local, mesh=mesh, in_specs=in_specs, out_specs=out_specs, check_vma=False)
```

```python
import functools

import jax
import jax.numpy as jnp
from jax import lax
from jax.experimental import pallas as pl
from jax.experimental.pallas import tpu as pltpu
from jax.sharding import PartitionSpec as P

TILE = 128
SUB = 8
EXTRA = 16
F32 = jnp.float32
BF16 = jnp.bfloat16
VMEM = pl.BlockSpec(memory_space=pltpu.VMEM)
SMEM = pl.BlockSpec(memory_space=pltpu.SMEM)


def call(body, out_shape, in_specs, scratch=(), megabytes=32, aliases=None, out_specs=None):
    many = isinstance(out_shape, (list, tuple))
    return pl.pallas_call(
        body,
        out_shape=out_shape,
        in_specs=in_specs,
        out_specs=out_specs or ([VMEM] * len(out_shape) if many else VMEM),
        scratch_shapes=list(scratch),
        compiler_params=pltpu.CompilerParams(vmem_limit_bytes=megabytes << 20),
        input_output_aliases=aliases or {},
        cost_estimate=pl.CostEstimate(flops=0, bytes_accessed=0, transcendentals=0),
    )


def iota(shape, dimension):
    return lax.broadcasted_iota(jnp.int32, shape, dimension)


def swap_matrix():
    target = iota((TILE, TILE), 1)
    h, a, b = target // (SUB * SUB), target // SUB % SUB, target % SUB
    return iota((TILE, TILE), 0) == (1 - h) * SUB * SUB + b * SUB + a


def pack_kernel(integrals_ref, blocks_ref, out_ref, sems):
    slabs, length = integrals_ref.shape[:2]
    copies = [
        pltpu.make_async_copy(integrals_ref.at[s], out_ref.at[s, pl.ds(0, length)], sems.at[s]) for s in range(slabs)
    ]
    for copy in copies:
        copy.start()
    lane = iota((EXTRA, TILE), 1)
    for s in range(slabs):
        ids = jnp.zeros((EXTRA, TILE), jnp.int32)
        for t in range(length // TILE):
            for which in range(2):
                ids = jnp.where(lane == 2 * t + which, blocks_ref[s, which, t], ids)
        out_ref[s, length:, :] = ids.astype(F32).astype(BF16)
    for copy in copies:
        copy.wait()


def cut_kernel(x_ref, y_ref, *outs):
    for s, out_ref in enumerate(outs):
        out_ref[...] = (x_ref if s % 2 == 0 else y_ref)[s]


def add_products(grid_ref, acc_refs, tiles_ref, blocks_ref):
    empty = jnp.zeros((TILE, TILE), BF16)

    @pl.loop(0, blocks_ref.shape[0] // 4, unroll=4)
    def _(t):
        to = [blocks_ref[4 * t + 2 * k] for k in range(2)]
        come = [blocks_ref[4 * t + 2 * k + 1] for k in range(2)]
        tiles = [tiles_ref[pl.ds(pl.multiple_of((2 * t + k) * TILE, TILE), TILE), :] for k in range(2)]
        left = jnp.concatenate([grid_ref[come[0]], grid_ref[come[1]]], axis=1)
        right = jnp.concatenate(
            [jnp.concatenate([tiles[0], empty], axis=1), jnp.concatenate([empty, tiles[1]], axis=1)], axis=0
        )
        products = jnp.dot(left, right, preferred_element_type=F32)
        for k in range(2):
            acc_refs[k][to[k]] += products[:, k * TILE : (k + 1) * TILE]


def first_kernel(n_vir, n_sets, *refs):
    own, other = refs[:n_vir], refs[n_vir : 2 * n_vir]
    tiles = refs[2 * n_vir : 2 * n_vir + n_sets]
    blocks = refs[2 * n_vir + n_sets : 2 * n_vir + 2 * n_sets]
    row_ref, column_ref, grid_ref, *acc_refs = refs[2 * n_vir + 2 * n_sets :]
    rows, width = own[0].shape
    per = width // TILE
    pair = lax.axis_index("pair")
    vir = lax.axis_index("vir")
    upper = pair % 2 == 1
    base = (pair ^ 1) * rows
    wanted = jnp.where(upper, row_ref[...] - base - iota((rows, rows), 0), column_ref[...] - base - iota((rows, rows), 1))
    hot = jnp.where(wanted == 0, 1.0, 0.0).astype(BF16)
    for shift in range(n_vir):
        first = (vir ^ shift) * per
        mine, others = own[shift][...], other[shift][...]
        kept = jnp.where(upper, others, mine)
        moved = jnp.dot(hot, jnp.where(upper, mine, others), preferred_element_type=F32).astype(BF16)
        for k in range(per):
            columns = slice(k * TILE, (k + 1) * TILE)
            grid_ref[first + k, :rows] = kept[:, columns]
            grid_ref[first + k, rows:] = moved[:, columns]
    for acc_ref in acc_refs:
        acc_ref[...] = jnp.zeros_like(acc_ref)
    for tiles_ref, blocks_ref in zip(tiles, blocks):
        for s in range(tiles_ref.shape[0]):
            add_products(grid_ref, acc_refs, tiles_ref.at[s], blocks_ref.at[s])


def second_kernel(n_vir, n_sets, *refs):
    grid_ref = refs[0]
    tiles, blocks = refs[3 : 3 + n_sets], refs[3 + n_sets : 3 + 2 * n_sets]
    keep_ref, send_ref, *acc_refs = refs[3 + 2 * n_sets :]
    half, rows = keep_ref.shape[1:3]
    core = lax.axis_index("pair") % 2
    vir = lax.axis_index("vir")
    for tiles_ref, blocks_ref in zip(tiles, blocks):
        for s in range(tiles_ref.shape[0]):
            add_products(grid_ref, acc_refs, tiles_ref.at[s], blocks_ref.at[s])
    swap = swap_matrix().astype(BF16)
    for shift in range(n_vir):
        for k in range(half):
            for out_ref, side in ((keep_ref, core), (send_ref, 1 - core)):
                block = ((vir ^ shift) * 2 + side) * half + k
                lower = acc_refs[0][block, :rows] + acc_refs[1][block, :rows]
                upper = (acc_refs[0][block, rows:] + acc_refs[1][block, rows:]).astype(BF16)
                out_ref[shift, k] = (lower + jnp.dot(upper, swap, preferred_element_type=F32)).astype(BF16)


def join_kernel(keep_ref, come_ref, *outs):
    for shift, out_ref in enumerate(outs):
        out_ref[...] = (keep_ref[shift].astype(F32) + come_ref[shift].astype(F32)).astype(BF16)


def total_kernel(*refs):
    total = refs[0][...].astype(F32)
    for ref in refs[1:-1]:
        total += ref[...].astype(F32)
    refs[-1][...] = total.astype(BF16)


def finish_kernel(own_ref, other_ref, column_ref, out_ref):
    half, rows, _ = own_ref.shape
    pair = lax.axis_index("pair")
    upper = pair % 2 == 1
    place = jnp.where(upper, column_ref[...] - (pair ^ 1) * rows, iota((rows, 1), 0))
    hot = (iota((rows, rows), 1) == place).astype(BF16)
    same = (iota((TILE, TILE), 0) == iota((TILE, TILE), 1)).astype(F32)
    swap = jnp.where(upper, swap_matrix().astype(F32), same).astype(BF16)
    for which in range(2):
        for k in range(half):
            values = jnp.where(upper == (which == 1), own_ref[k], other_ref[k])
            values = jnp.dot(values, swap, preferred_element_type=F32).astype(BF16)
            column = (which * half + k) * TILE
            out_ref[:, column : column + TILE] = jnp.dot(hot, values, preferred_element_type=F32).astype(BF16)


def local(amplitudes, integrals, tile_blocks, mirror_row):
    rows, width = amplitudes.shape
    slabs, tile_dev = integrals.shape[:2]
    n_pair, n_vir = lax.axis_size("pair"), lax.axis_size("vir")
    chips = n_pair // 2
    per = width // TILE
    n_blk = per * n_vir
    length = tile_dev * TILE

    def across(array, bits):
        return lax.ppermute(array, "pair", [(i, i ^ bits) for i in range(n_pair)])

    def along(array, bits):
        return lax.ppermute(array, "vir", [(i, i ^ bits) for i in range(n_vir)])

    packed = call(
        pack_kernel,
        jax.ShapeDtypeStruct((slabs, length + EXTRA, TILE), BF16),
        [pl.BlockSpec(memory_space=pltpu.HBM), SMEM],
        [pltpu.SemaphoreType.DMA((slabs,))],
        megabytes=8,
    )(integrals.reshape(slabs, length, TILE), tile_blocks.transpose(0, 2, 1))
    early = [packed, across(packed, 2), across(packed, 4)]

    pieces = {0: amplitudes}
    reach = n_vir // 2
    while reach:
        pieces |= {shift + reach: along(piece, reach) for shift, piece in pieces.items()}
        reach //= 2
    mine = [pieces[shift] for shift in range(n_vir)]
    others = [across(piece, 1) for piece in mine]
    tiles_x, tiles_y, *_ = lax.optimization_barrier((*early[1:], *others[:2], *mine[:-1]))
    slab = jax.ShapeDtypeStruct((length + EXTRA, TILE), BF16)
    halves = call(cut_kernel, [slab] * slabs, [VMEM, VMEM], megabytes=8)(tiles_x, tiles_y)
    late = [across(half, 4 if s % 2 == 0 else 2) for s, half in enumerate(halves)]
    reach = 4
    while reach < chips:
        farther = early + late if reach == 4 else late
        late = late + [across(array, 2 * reach) for array in farther]
        reach *= 2
    late = [array.reshape(-1, length + EXTRA, TILE) for array in late]
    row, column = mirror_row.reshape(1, rows), mirror_row.reshape(rows, 1)

    def ids(array):
        return array[:, length, : 2 * tile_dev].astype(jnp.int32)

    sums = jax.ShapeDtypeStruct((n_blk, 2 * rows, TILE), F32)
    grid, *sums_so_far = call(
        functools.partial(first_kernel, n_vir, len(early)),
        [jax.ShapeDtypeStruct((n_blk, 2 * rows, TILE), BF16), sums, sums],
        [VMEM] * (2 * n_vir + len(early)) + [SMEM] * len(early) + [VMEM, VMEM],
        megabytes=32,
    )(*mine, *others, *early, *[ids(array) for array in early], row, column)
    piece = jax.ShapeDtypeStruct((n_vir, per // 2, rows, TILE), BF16)
    keep, send, *_ = call(
        functools.partial(second_kernel, n_vir, len(late)),
        [piece, piece, sums, sums],
        [VMEM] * (3 + len(late)) + [SMEM] * len(late),
        megabytes=32,
        aliases={1: 2, 2: 3},
    )(grid, *sums_so_far, *late, *[ids(array) for array in late])
    one = jax.ShapeDtypeStruct((per // 2, rows, TILE), BF16)
    parts = call(join_kernel, [one] * n_vir, [VMEM, VMEM], megabytes=8)(keep, across(send, 1))
    parts = dict(enumerate(parts))
    reach, arrived = 1, []
    while reach < n_vir:
        far = {shift: along(parts[shift], reach) for shift in parts if shift & reach and shift > reach}
        for shift, array in far.items():
            parts[shift ^ reach] = call(total_kernel, one, [VMEM] * 2, megabytes=8)(parts[shift ^ reach], array)
        near, *_ = lax.optimization_barrier((parts[reach], *far.values()))
        arrived.append(along(near, reach))
        parts = {shift: part for shift, part in parts.items() if not shift & reach}
        reach *= 2
    total = call(total_kernel, one, [VMEM] * (1 + len(arrived)), megabytes=8)(parts[0], *arrived)
    return call(
        finish_kernel, jax.ShapeDtypeStruct((rows, width), BF16), [VMEM] * 3, megabytes=8
    )(total, across(total, 1), column)


def solution(mesh):
    in_specs = (
        P("pair", "vir"),
        P(None, ("pair", "vir"), None, None),
        P(None, ("pair", "vir"), None),
        P("pair"),
    )
    out_specs = P("pair", "vir")
    return jax.shard_map(local, mesh=mesh, in_specs=in_specs, out_specs=out_specs, check_vma=False)
```

```python
import functools

import jax
import jax.numpy as jnp
from jax import lax
from jax.experimental import pallas as pl
from jax.experimental.pallas import tpu as pltpu
from jax.sharding import PartitionSpec as P

TILE = 128
SUB = 8
EXTRA = 16
F32 = jnp.float32
BF16 = jnp.bfloat16
VMEM = pl.BlockSpec(memory_space=pltpu.VMEM)
SMEM = pl.BlockSpec(memory_space=pltpu.SMEM)


def call(body, out_shape, in_specs, scratch=(), megabytes=32, aliases=None, out_specs=None):
    many = isinstance(out_shape, (list, tuple))
    return pl.pallas_call(
        body,
        out_shape=out_shape,
        in_specs=in_specs,
        out_specs=out_specs or ([VMEM] * len(out_shape) if many else VMEM),
        scratch_shapes=list(scratch),
        compiler_params=pltpu.CompilerParams(vmem_limit_bytes=megabytes << 20),
        input_output_aliases=aliases or {},
        cost_estimate=pl.CostEstimate(flops=0, bytes_accessed=0, transcendentals=0),
    )


def iota(shape, dimension):
    return lax.broadcasted_iota(jnp.int32, shape, dimension)


def swap_matrix():
    target = iota((TILE, TILE), 1)
    h, a, b = target // (SUB * SUB), target // SUB % SUB, target % SUB
    return iota((TILE, TILE), 0) == (1 - h) * SUB * SUB + b * SUB + a


def pack_kernel(integrals_ref, blocks_ref, out_ref, sems):
    slabs, length = integrals_ref.shape[:2]
    copies = [
        pltpu.make_async_copy(integrals_ref.at[s], out_ref.at[s, pl.ds(0, length)], sems.at[s]) for s in range(slabs)
    ]
    for copy in copies:
        copy.start()
    lane = iota((EXTRA, TILE), 1)
    for s in range(slabs):
        ids = jnp.zeros((EXTRA, TILE), jnp.int32)
        for t in range(length // TILE):
            for which in range(2):
                ids = jnp.where(lane == 2 * t + which, blocks_ref[s, which, t], ids)
        out_ref[s, length:, :] = ids.astype(F32).astype(BF16)
    for copy in copies:
        copy.wait()


def cut_kernel(x_ref, y_ref, *outs):
    for s, out_ref in enumerate(outs):
        out_ref[...] = (x_ref if s % 2 == 0 else y_ref)[s]


def add_products(grid_ref, acc_refs, tiles_ref, blocks_ref):
    empty = jnp.zeros((TILE, TILE), BF16)

    @pl.loop(0, blocks_ref.shape[0] // 4, unroll=4)
    def _(t):
        to = [blocks_ref[4 * t + 2 * k] for k in range(2)]
        come = [blocks_ref[4 * t + 2 * k + 1] for k in range(2)]
        tiles = [tiles_ref[pl.ds(pl.multiple_of((2 * t + k) * TILE, TILE), TILE), :] for k in range(2)]
        left = jnp.concatenate([grid_ref[come[0]], grid_ref[come[1]]], axis=1)
        right = jnp.concatenate(
            [jnp.concatenate([tiles[0], empty], axis=1), jnp.concatenate([empty, tiles[1]], axis=1)], axis=0
        )
        products = jnp.dot(left, right, preferred_element_type=F32)
        for k in range(2):
            acc_refs[k][to[k]] += products[:, k * TILE : (k + 1) * TILE]


def first_kernel(n_vir, n_sets, *refs):
    own, other = refs[:n_vir], refs[n_vir : 2 * n_vir]
    tiles = refs[2 * n_vir : 2 * n_vir + n_sets]
    blocks = refs[2 * n_vir + n_sets : 2 * n_vir + 2 * n_sets]
    row_ref, column_ref, grid_ref, *acc_refs = refs[2 * n_vir + 2 * n_sets :]
    rows, width = own[0].shape
    per = width // TILE
    pair = lax.axis_index("pair")
    vir = lax.axis_index("vir")
    upper = pair % 2 == 1
    base = (pair ^ 1) * rows
    wanted = jnp.where(upper, row_ref[...] - base - iota((rows, rows), 0), column_ref[...] - base - iota((rows, rows), 1))
    hot = jnp.where(wanted == 0, 1.0, 0.0).astype(BF16)
    for shift in range(n_vir):
        first = (vir ^ shift) * per
        mine, others = own[shift][...], other[shift][...]
        kept = jnp.where(upper, others, mine)
        moved = jnp.dot(hot, jnp.where(upper, mine, others), preferred_element_type=F32).astype(BF16)
        for k in range(per):
            columns = slice(k * TILE, (k + 1) * TILE)
            grid_ref[first + k, :rows] = kept[:, columns]
            grid_ref[first + k, rows:] = moved[:, columns]
    for acc_ref in acc_refs:
        acc_ref[...] = jnp.zeros_like(acc_ref)
    for tiles_ref, blocks_ref in zip(tiles, blocks):
        for s in range(tiles_ref.shape[0]):
            add_products(grid_ref, acc_refs, tiles_ref.at[s], blocks_ref.at[s])


def second_kernel(n_vir, n_sets, *refs):
    grid_ref = refs[0]
    tiles, blocks = refs[3 : 3 + n_sets], refs[3 + n_sets : 3 + 2 * n_sets]
    keep_ref, send_ref, *acc_refs = refs[3 + 2 * n_sets :]
    half, rows = keep_ref.shape[1:3]
    core = lax.axis_index("pair") % 2
    vir = lax.axis_index("vir")
    for tiles_ref, blocks_ref in zip(tiles, blocks):
        for s in range(tiles_ref.shape[0]):
            add_products(grid_ref, acc_refs, tiles_ref.at[s], blocks_ref.at[s])
    swap = swap_matrix().astype(BF16)
    for shift in range(n_vir):
        for k in range(half):
            for out_ref, side in ((keep_ref, core), (send_ref, 1 - core)):
                block = ((vir ^ shift) * 2 + side) * half + k
                lower = acc_refs[0][block, :rows] + acc_refs[1][block, :rows]
                upper = (acc_refs[0][block, rows:] + acc_refs[1][block, rows:]).astype(BF16)
                out_ref[shift, k] = (lower + jnp.dot(upper, swap, preferred_element_type=F32)).astype(BF16)


def join_kernel(keep_ref, come_ref, *outs):
    for shift, out_ref in enumerate(outs):
        out_ref[...] = (keep_ref[shift].astype(F32) + come_ref[shift].astype(F32)).astype(BF16)


def total_kernel(*refs):
    total = refs[0][...].astype(F32)
    for ref in refs[1:-1]:
        total += ref[...].astype(F32)
    refs[-1][...] = total.astype(BF16)


def finish_kernel(own_ref, other_ref, column_ref, out_ref):
    half, rows, _ = own_ref.shape
    pair = lax.axis_index("pair")
    upper = pair % 2 == 1
    place = jnp.where(upper, column_ref[...] - (pair ^ 1) * rows, iota((rows, 1), 0))
    hot = (iota((rows, rows), 1) == place).astype(BF16)
    same = (iota((TILE, TILE), 0) == iota((TILE, TILE), 1)).astype(F32)
    swap = jnp.where(upper, swap_matrix().astype(F32), same).astype(BF16)
    for which in range(2):
        for k in range(half):
            values = jnp.where(upper == (which == 1), own_ref[k], other_ref[k])
            values = jnp.dot(values, swap, preferred_element_type=F32).astype(BF16)
            column = (which * half + k) * TILE
            out_ref[:, column : column + TILE] = jnp.dot(hot, values, preferred_element_type=F32).astype(BF16)


def local(amplitudes, integrals, tile_blocks, mirror_row):
    rows, width = amplitudes.shape
    slabs, tile_dev = integrals.shape[:2]
    n_pair, n_vir = lax.axis_size("pair"), lax.axis_size("vir")
    chips = n_pair // 2
    per = width // TILE
    n_blk = per * n_vir
    length = tile_dev * TILE

    def across(array, bits):
        return lax.ppermute(array, "pair", [(i, i ^ bits) for i in range(n_pair)])

    def along(array, bits):
        return lax.ppermute(array, "vir", [(i, i ^ bits) for i in range(n_vir)])

    packed = call(
        pack_kernel,
        jax.ShapeDtypeStruct((slabs, length + EXTRA, TILE), BF16),
        [pl.BlockSpec(memory_space=pltpu.HBM), SMEM],
        [pltpu.SemaphoreType.DMA((slabs,))],
        megabytes=8,
    )(integrals.reshape(slabs, length, TILE), tile_blocks.transpose(0, 2, 1))
    early = [packed, across(packed, 2), across(packed, 4)]

    pieces = {0: amplitudes}
    reach = n_vir // 2
    while reach:
        pieces |= {shift + reach: along(piece, reach) for shift, piece in pieces.items()}
        reach //= 2
    mine = [pieces[shift] for shift in range(n_vir)]
    others = [across(piece, 1) for piece in mine]
    tiles_x, tiles_y, *_ = lax.optimization_barrier((*early[1:], *others[:-1], *mine[:-1]))
    slab = jax.ShapeDtypeStruct((length + EXTRA, TILE), BF16)
    halves = call(cut_kernel, [slab] * slabs, [VMEM, VMEM], megabytes=4)(tiles_x, tiles_y)
    late = [across(half, 4 if s % 2 == 0 else 2) for s, half in enumerate(halves)]
    reach = 4
    while reach < chips:
        farther = early + late if reach == 4 else late
        late = late + [across(array, 2 * reach) for array in farther]
        reach *= 2
    late = [array.reshape(-1, length + EXTRA, TILE) for array in late]
    row, column = mirror_row.reshape(1, rows), mirror_row.reshape(rows, 1)

    def ids(array):
        return array[:, length, : 2 * tile_dev].astype(jnp.int32)

    sums = jax.ShapeDtypeStruct((n_blk, 2 * rows, TILE), F32)
    grid, *sums_so_far = call(
        functools.partial(first_kernel, n_vir, len(early)),
        [jax.ShapeDtypeStruct((n_blk, 2 * rows, TILE), BF16), sums, sums],
        [VMEM] * (2 * n_vir + len(early)) + [SMEM] * len(early) + [VMEM, VMEM],
        megabytes=20,
    )(*mine, *others, *early, *[ids(array) for array in early], row, column)
    piece = jax.ShapeDtypeStruct((n_vir, per // 2, rows, TILE), BF16)
    keep, send, *_ = call(
        functools.partial(second_kernel, n_vir, len(late)),
        [piece, piece, sums, sums],
        [VMEM] * (3 + len(late)) + [SMEM] * len(late),
        megabytes=24,
        aliases={1: 2, 2: 3},
    )(grid, *sums_so_far, *late, *[ids(array) for array in late])
    one = jax.ShapeDtypeStruct((per // 2, rows, TILE), BF16)
    parts = call(join_kernel, [one] * n_vir, [VMEM, VMEM], megabytes=4)(keep, across(send, 1))
    arrived = [along(parts[shift], shift) for shift in range(n_vir - 1, 0, -1)]
    total = call(total_kernel, one, [VMEM] * n_vir, megabytes=4)(parts[0], *arrived)
    return call(
        finish_kernel, jax.ShapeDtypeStruct((rows, width), BF16), [VMEM] * 3, megabytes=8
    )(total, across(total, 1), column)


def solution(mesh):
    in_specs = (
        P("pair", "vir"),
        P(None, ("pair", "vir"), None, None),
        P(None, ("pair", "vir"), None),
        P("pair"),
    )
    out_specs = P("pair", "vir")
    return jax.shard_map(local, mesh=mesh, in_specs=in_specs, out_specs=out_specs, check_vma=False)
```

```python
import functools

import jax
import jax.numpy as jnp
from jax import lax
from jax.experimental import pallas as pl
from jax.experimental.pallas import tpu as pltpu
from jax.sharding import PartitionSpec as P

TILE = 128
SUB = 8
EXTRA = 16
F32 = jnp.float32
BF16 = jnp.bfloat16
VMEM = pl.BlockSpec(memory_space=pltpu.VMEM)
SMEM = pl.BlockSpec(memory_space=pltpu.SMEM)


def call(body, out_shape, in_specs, scratch=(), megabytes=32, aliases=None, out_specs=None):
    many = isinstance(out_shape, (list, tuple))
    return pl.pallas_call(
        body,
        out_shape=out_shape,
        in_specs=in_specs,
        out_specs=out_specs or ([VMEM] * len(out_shape) if many else VMEM),
        scratch_shapes=list(scratch),
        compiler_params=pltpu.CompilerParams(vmem_limit_bytes=megabytes << 20),
        input_output_aliases=aliases or {},
        cost_estimate=pl.CostEstimate(flops=0, bytes_accessed=0, transcendentals=0),
    )


def iota(shape, dimension):
    return lax.broadcasted_iota(jnp.int32, shape, dimension)


def swap_matrix():
    target = iota((TILE, TILE), 1)
    h, a, b = target // (SUB * SUB), target // SUB % SUB, target % SUB
    return iota((TILE, TILE), 0) == (1 - h) * SUB * SUB + b * SUB + a


def pack_kernel(integrals_ref, blocks_ref, out_ref, sems):
    slabs, length = integrals_ref.shape[:2]
    copies = [
        pltpu.make_async_copy(integrals_ref.at[s], out_ref.at[s, pl.ds(0, length)], sems.at[s]) for s in range(slabs)
    ]
    for copy in copies:
        copy.start()
    lane = iota((EXTRA, TILE), 1)
    for s in range(slabs):
        ids = jnp.zeros((EXTRA, TILE), jnp.int32)
        for t in range(length // TILE):
            for which in range(2):
                ids = jnp.where(lane == 2 * t + which, blocks_ref[s, which, t], ids)
        out_ref[s, length:, :] = ids.astype(F32).astype(BF16)
    for copy in copies:
        copy.wait()


def cut_kernel(x_ref, y_ref, *outs):
    for s, out_ref in enumerate(outs):
        out_ref[...] = (x_ref if s % 2 == 0 else y_ref)[s]


def add_products(grid_ref, acc_refs, tiles_ref, blocks_ref):
    empty = jnp.zeros((TILE, TILE), BF16)
    rows = acc_refs[0].shape[1]

    @pl.loop(0, blocks_ref.shape[0] // 4, unroll=4)
    def _(t):
        to = [blocks_ref[4 * t + 2 * k] for k in range(2)]
        come = [blocks_ref[4 * t + 2 * k + 1] for k in range(2)]
        tiles = [tiles_ref[pl.ds(pl.multiple_of((2 * t + k) * TILE, TILE), TILE), :] for k in range(2)]
        right = jnp.concatenate(
            [jnp.concatenate([tiles[0], empty], axis=1), jnp.concatenate([empty, tiles[1]], axis=1)], axis=0
        )
        products = []
        for side in range(2):
            part = slice(side * rows, (side + 1) * rows)
            left = jnp.concatenate([grid_ref[come[0], part], grid_ref[come[1], part]], axis=1)
            products.append(jnp.dot(left, right, preferred_element_type=F32))
        for k in range(2):
            for side in range(2):
                acc_refs[side][to[k]] += products[side][:, k * TILE : (k + 1) * TILE]


def first_kernel(n_vir, n_sets, *refs):
    own, other = refs[:n_vir], refs[n_vir : 2 * n_vir]
    tiles = refs[2 * n_vir : 2 * n_vir + n_sets]
    blocks = refs[2 * n_vir + n_sets : 2 * n_vir + 2 * n_sets]
    row_ref, column_ref, grid_ref, *acc_refs = refs[2 * n_vir + 2 * n_sets :]
    rows, width = own[0].shape
    per = width // TILE
    pair = lax.axis_index("pair")
    vir = lax.axis_index("vir")
    upper = pair % 2 == 1
    base = (pair ^ 1) * rows
    wanted = jnp.where(upper, row_ref[...] - base - iota((rows, rows), 0), column_ref[...] - base - iota((rows, rows), 1))
    hot = jnp.where(wanted == 0, 1.0, 0.0).astype(BF16)
    for shift in range(n_vir):
        first = (vir ^ shift) * per
        mine, others = own[shift][...], other[shift][...]
        kept = jnp.where(upper, others, mine)
        moved = jnp.dot(hot, jnp.where(upper, mine, others), preferred_element_type=F32).astype(BF16)
        for k in range(per):
            columns = slice(k * TILE, (k + 1) * TILE)
            grid_ref[first + k, :rows] = kept[:, columns]
            grid_ref[first + k, rows:] = moved[:, columns]
    for acc_ref in acc_refs:
        acc_ref[...] = jnp.zeros_like(acc_ref)
    for tiles_ref, blocks_ref in zip(tiles, blocks):
        for s in range(tiles_ref.shape[0]):
            add_products(grid_ref, acc_refs, tiles_ref.at[s], blocks_ref.at[s])


def second_kernel(n_vir, n_sets, *refs):
    grid_ref = refs[0]
    tiles, blocks = refs[3 : 3 + n_sets], refs[3 + n_sets : 3 + 2 * n_sets]
    keep_ref, send_ref, *acc_refs = refs[3 + 2 * n_sets :]
    half, rows = keep_ref.shape[1:3]
    core = lax.axis_index("pair") % 2
    vir = lax.axis_index("vir")
    for tiles_ref, blocks_ref in zip(tiles, blocks):
        for s in range(tiles_ref.shape[0]):
            add_products(grid_ref, acc_refs, tiles_ref.at[s], blocks_ref.at[s])
    swap = swap_matrix().astype(BF16)
    for shift in range(n_vir):
        for k in range(half):
            for out_ref, side in ((keep_ref, core), (send_ref, 1 - core)):
                block = ((vir ^ shift) * 2 + side) * half + k
                upper = acc_refs[1][block].astype(BF16)
                total = acc_refs[0][block] + jnp.dot(upper, swap, preferred_element_type=F32)
                out_ref[shift, k] = total.astype(BF16)


def join_kernel(keep_ref, come_ref, *outs):
    for shift, out_ref in enumerate(outs):
        out_ref[...] = (keep_ref[shift].astype(F32) + come_ref[shift].astype(F32)).astype(BF16)


def total_kernel(*refs):
    total = refs[0][...].astype(F32)
    for ref in refs[1:-1]:
        total += ref[...].astype(F32)
    refs[-1][...] = total.astype(BF16)


def finish_kernel(own_ref, other_ref, column_ref, out_ref):
    half, rows, _ = own_ref.shape
    pair = lax.axis_index("pair")
    upper = pair % 2 == 1
    place = jnp.where(upper, column_ref[...] - (pair ^ 1) * rows, iota((rows, 1), 0))
    hot = (iota((rows, rows), 1) == place).astype(BF16)
    same = (iota((TILE, TILE), 0) == iota((TILE, TILE), 1)).astype(F32)
    swap = jnp.where(upper, swap_matrix().astype(F32), same).astype(BF16)
    for which in range(2):
        for k in range(half):
            values = jnp.where(upper == (which == 1), own_ref[k], other_ref[k])
            values = jnp.dot(values, swap, preferred_element_type=F32).astype(BF16)
            column = (which * half + k) * TILE
            out_ref[:, column : column + TILE] = jnp.dot(hot, values, preferred_element_type=F32).astype(BF16)


def local(amplitudes, integrals, tile_blocks, mirror_row):
    rows, width = amplitudes.shape
    slabs, tile_dev = integrals.shape[:2]
    n_pair, n_vir = lax.axis_size("pair"), lax.axis_size("vir")
    chips = n_pair // 2
    per = width // TILE
    n_blk = per * n_vir
    length = tile_dev * TILE

    def across(array, bits):
        return lax.ppermute(array, "pair", [(i, i ^ bits) for i in range(n_pair)])

    def along(array, bits):
        return lax.ppermute(array, "vir", [(i, i ^ bits) for i in range(n_vir)])

    packed = call(
        pack_kernel,
        jax.ShapeDtypeStruct((slabs, length + EXTRA, TILE), BF16),
        [pl.BlockSpec(memory_space=pltpu.HBM), SMEM],
        [pltpu.SemaphoreType.DMA((slabs,))],
        megabytes=8,
    )(integrals.reshape(slabs, length, TILE), tile_blocks.transpose(0, 2, 1))
    early = [packed, across(packed, 2), across(packed, 4)]

    pieces = {0: amplitudes}
    reach = n_vir // 2
    while reach:
        pieces |= {shift + reach: along(piece, reach) for shift, piece in pieces.items()}
        reach //= 2
    mine = [pieces[shift] for shift in range(n_vir)]
    others = [across(piece, 1) for piece in mine]
    tiles_x, tiles_y, *_ = lax.optimization_barrier((*early[1:], *others[:-1], *mine[:-1]))
    slab = jax.ShapeDtypeStruct((length + EXTRA, TILE), BF16)
    halves = call(cut_kernel, [slab] * slabs, [VMEM, VMEM], megabytes=4)(tiles_x, tiles_y)
    late = [across(half, 4 if s % 2 == 0 else 2) for s, half in enumerate(halves)]
    reach = 4
    while reach < chips:
        farther = early + late if reach == 4 else late
        late = late + [across(array, 2 * reach) for array in farther]
        reach *= 2
    late = [array.reshape(-1, length + EXTRA, TILE) for array in late]
    row, column = mirror_row.reshape(1, rows), mirror_row.reshape(rows, 1)

    def ids(array):
        return array[:, length, : 2 * tile_dev].astype(jnp.int32)

    sums = jax.ShapeDtypeStruct((n_blk, rows, TILE), F32)
    grid, *sums_so_far = call(
        functools.partial(first_kernel, n_vir, len(early)),
        [jax.ShapeDtypeStruct((n_blk, 2 * rows, TILE), BF16), sums, sums],
        [VMEM] * (2 * n_vir + len(early)) + [SMEM] * len(early) + [VMEM, VMEM],
        megabytes=20,
    )(*mine, *others, *early, *[ids(array) for array in early], row, column)
    piece = jax.ShapeDtypeStruct((n_vir, per // 2, rows, TILE), BF16)
    keep, send, *_ = call(
        functools.partial(second_kernel, n_vir, len(late)),
        [piece, piece, sums, sums],
        [VMEM] * (3 + len(late)) + [SMEM] * len(late),
        megabytes=24,
        aliases={1: 2, 2: 3},
    )(grid, *sums_so_far, *late, *[ids(array) for array in late])
    one = jax.ShapeDtypeStruct((per // 2, rows, TILE), BF16)
    parts = call(join_kernel, [one] * n_vir, [VMEM, VMEM], megabytes=4)(keep, across(send, 1))
    arrived = [along(parts[shift], shift) for shift in range(n_vir - 1, 0, -1)]
    total = call(total_kernel, one, [VMEM] * n_vir, megabytes=4)(parts[0], *arrived)
    return call(
        finish_kernel, jax.ShapeDtypeStruct((rows, width), BF16), [VMEM] * 3, megabytes=8
    )(total, across(total, 1), column)


def solution(mesh):
    in_specs = (
        P("pair", "vir"),
        P(None, ("pair", "vir"), None, None),
        P(None, ("pair", "vir"), None),
        P("pair"),
    )
    out_specs = P("pair", "vir")
    return jax.shard_map(local, mesh=mesh, in_specs=in_specs, out_specs=out_specs, check_vma=False)
```

```python
import functools

import jax
import jax.numpy as jnp
from jax import lax
from jax.experimental import pallas as pl
from jax.experimental.pallas import tpu as pltpu
from jax.sharding import PartitionSpec as P

TILE = 128
SUB = 8
EXTRA = 16
F32 = jnp.float32
BF16 = jnp.bfloat16
VMEM = pl.BlockSpec(memory_space=pltpu.VMEM)
SMEM = pl.BlockSpec(memory_space=pltpu.SMEM)


def call(body, out_shape, in_specs, scratch=(), megabytes=32, aliases=None, out_specs=None):
    many = isinstance(out_shape, (list, tuple))
    return pl.pallas_call(
        body,
        out_shape=out_shape,
        in_specs=in_specs,
        out_specs=out_specs or ([VMEM] * len(out_shape) if many else VMEM),
        scratch_shapes=list(scratch),
        compiler_params=pltpu.CompilerParams(vmem_limit_bytes=megabytes << 20),
        input_output_aliases=aliases or {},
        cost_estimate=pl.CostEstimate(flops=0, bytes_accessed=0, transcendentals=0),
    )


def iota(shape, dimension):
    return lax.broadcasted_iota(jnp.int32, shape, dimension)


def swap_matrix():
    target = iota((TILE, TILE), 1)
    h, a, b = target // (SUB * SUB), target // SUB % SUB, target % SUB
    return iota((TILE, TILE), 0) == (1 - h) * SUB * SUB + b * SUB + a


def cut_kernel(slabs, x_ref, y_ref, *refs):
    for s, out_ref in enumerate(refs[-slabs:]):
        out_ref[...] = (x_ref if s % 2 == 0 else y_ref)[s]


def add_products(grid_ref, acc_refs, tiles_ref, blocks_ref):
    empty = jnp.zeros((TILE, TILE), BF16)
    rows = acc_refs[0].shape[1]

    @pl.loop(0, blocks_ref.shape[1] // 2, unroll=4)
    def _(t):
        to, come = [[blocks_ref[which, 2 * t + k] for k in range(2)] for which in range(2)]
        tiles = [tiles_ref[pl.ds(pl.multiple_of((2 * t + k) * TILE, TILE), TILE), :] for k in range(2)]
        right = jnp.concatenate(
            [jnp.concatenate([tiles[0], empty], axis=1), jnp.concatenate([empty, tiles[1]], axis=1)], axis=0
        )
        products = []
        for side in range(2):
            part = slice(side * rows, (side + 1) * rows)
            left = jnp.concatenate([grid_ref[come[0], part], grid_ref[come[1], part]], axis=1)
            products.append(jnp.dot(left, right, preferred_element_type=F32))
        for k in range(2):
            for side in range(2):
                acc_refs[side][to[k]] += products[side][:, k * TILE : (k + 1) * TILE]


def first_kernel(n_vir, n_sets, *refs):
    own, other = refs[:n_vir], refs[n_vir : 2 * n_vir]
    tiles = refs[2 * n_vir : 2 * n_vir + n_sets]
    blocks = refs[2 * n_vir + n_sets : 2 * n_vir + 2 * n_sets]
    row_ref, column_ref, grid_ref, *acc_refs = refs[2 * n_vir + 2 * n_sets :]
    rows, width = own[0].shape
    per = width // TILE
    pair = lax.axis_index("pair")
    vir = lax.axis_index("vir")
    upper = pair % 2 == 1
    base = (pair ^ 1) * rows
    wanted = jnp.where(upper, row_ref[...] - base - iota((rows, rows), 0), column_ref[...] - base - iota((rows, rows), 1))
    hot = jnp.where(wanted == 0, 1.0, 0.0).astype(BF16)
    for shift in range(n_vir):
        first = (vir ^ shift) * per
        mine, others = own[shift][...], other[shift][...]
        kept = jnp.where(upper, others, mine)
        moved = jnp.dot(hot, jnp.where(upper, mine, others), preferred_element_type=F32).astype(BF16)
        for k in range(per):
            columns = slice(k * TILE, (k + 1) * TILE)
            grid_ref[first + k, :rows] = kept[:, columns]
            grid_ref[first + k, rows:] = moved[:, columns]
    for acc_ref in acc_refs:
        acc_ref[...] = jnp.zeros_like(acc_ref)
    for tiles_ref, blocks_ref in zip(tiles, blocks):
        for s in range(tiles_ref.shape[0]):
            add_products(grid_ref, acc_refs, tiles_ref.at[s], blocks_ref.at[s])


def second_kernel(n_vir, n_sets, *refs):
    grid_ref = refs[0]
    tiles, blocks = refs[3 : 3 + n_sets], refs[3 + n_sets : 3 + 2 * n_sets]
    keep_ref, send_ref, *acc_refs = refs[3 + 2 * n_sets :]
    half, rows = keep_ref.shape[1:3]
    core = lax.axis_index("pair") % 2
    vir = lax.axis_index("vir")
    for tiles_ref, blocks_ref in zip(tiles, blocks):
        for s in range(tiles_ref.shape[0]):
            add_products(grid_ref, acc_refs, tiles_ref.at[s], blocks_ref.at[s])
    swap = swap_matrix().astype(BF16)
    for shift in range(n_vir):
        for k in range(half):
            for out_ref, side in ((keep_ref, core), (send_ref, 1 - core)):
                block = ((vir ^ shift) * 2 + side) * half + k
                upper = acc_refs[1][block].astype(BF16)
                total = acc_refs[0][block] + jnp.dot(upper, swap, preferred_element_type=F32)
                out_ref[shift, k] = total.astype(BF16)


def join_kernel(keep_ref, come_ref, *outs):
    for place in range(keep_ref.shape[0]):
        total = keep_ref[place].astype(F32) + come_ref[place].astype(F32)
        outs[place % 2][place // 2] = total.astype(BF16)


def finish_kernel(own_ref, other_ref, column_ref, out_ref):
    half, rows, _ = own_ref.shape
    pair = lax.axis_index("pair")
    upper = pair % 2 == 1
    place = jnp.where(upper, column_ref[...] - (pair ^ 1) * rows, iota((rows, 1), 0))
    hot = (iota((rows, rows), 1) == place).astype(BF16)
    same = (iota((TILE, TILE), 0) == iota((TILE, TILE), 1)).astype(F32)
    swap = jnp.where(upper, swap_matrix().astype(F32), same).astype(BF16)
    for which in range(2):
        for k in range(half):
            values = jnp.where(upper == (which == 1), own_ref[k], other_ref[k])
            values = jnp.dot(values, swap, preferred_element_type=F32).astype(BF16)
            column = (which * half + k) * TILE
            out_ref[:, column : column + TILE] = jnp.dot(hot, values, preferred_element_type=F32).astype(BF16)


def local(amplitudes, integrals, tile_blocks, mirror_row):
    rows, width = amplitudes.shape
    slabs, tile_dev = integrals.shape[:2]
    n_pair, n_vir = lax.axis_size("pair"), lax.axis_size("vir")
    chips = n_pair // 2
    per = width // TILE
    n_blk = per * n_vir
    length = tile_dev * TILE

    def across(array, bits):
        return lax.ppermute(array, "pair", [(i, i ^ bits) for i in range(n_pair)])

    def along(array, bits):
        return lax.ppermute(array, "vir", [(i, i ^ bits) for i in range(n_vir)])

    ids = tile_blocks.transpose(0, 2, 1).astype(BF16)
    ids = jnp.pad(ids, ((0, 0), (0, EXTRA - 2), (0, TILE - tile_dev)))
    packed = jnp.concatenate([integrals.reshape(slabs, length, TILE), ids], axis=1)
    early = [packed, across(packed, 2), across(packed, 4)]

    pieces = {0: amplitudes}
    reach = n_vir // 2
    while reach:
        pieces |= {shift + reach: along(piece, reach) for shift, piece in pieces.items()}
        reach //= 2
    mine = [pieces[shift] for shift in range(n_vir)]
    others = [across(piece, 1) for piece in mine]
    first = [*others[:-1], *mine[1:-1]]
    slab = jax.ShapeDtypeStruct((length + EXTRA, TILE), BF16)
    halves = call(
        functools.partial(cut_kernel, slabs),
        [slab] * slabs,
        [VMEM, VMEM] + [pl.BlockSpec(memory_space=pl.ANY)] * len(first),
        megabytes=4,
    )(early[1], early[2], *first)
    late = [across(half, 4 if s % 2 == 0 else 2) for s, half in enumerate(halves)]
    reach = 4
    while reach < chips:
        farther = early + late if reach == 4 else late
        late = late + [across(array, 2 * reach) for array in farther]
        reach *= 2
    late = [array.reshape(-1, length + EXTRA, TILE) for array in late]
    row, column = mirror_row.reshape(1, rows), mirror_row.reshape(rows, 1)

    def ids(array):
        return array[:, length : length + 2, :tile_dev].astype(jnp.int32)

    sums = jax.ShapeDtypeStruct((n_blk, rows, TILE), F32)
    grid, *sums_so_far = call(
        functools.partial(first_kernel, n_vir, len(early)),
        [jax.ShapeDtypeStruct((n_blk, 2 * rows, TILE), BF16), sums, sums],
        [VMEM] * (2 * n_vir + len(early)) + [SMEM] * len(early) + [VMEM, VMEM],
        megabytes=20,
    )(*mine, *others, *early, *[ids(array) for array in early], row, column)
    piece = jax.ShapeDtypeStruct((n_vir, per // 2, rows, TILE), BF16)
    keep, send, *_ = call(
        functools.partial(second_kernel, n_vir, len(late)),
        [piece, piece, sums, sums],
        [VMEM] * (3 + len(late)) + [SMEM] * len(late),
        megabytes=24,
        aliases={1: 2, 2: 3},
    )(grid, *sums_so_far, *late, *[ids(array) for array in late])
    come, left, reach = across(send, 1), n_vir, 1
    while left > 1:
        left //= 2
        part = jax.ShapeDtypeStruct((left, per // 2, rows, TILE), BF16)
        keep, send = call(join_kernel, [part, part], [VMEM, VMEM], megabytes=4)(keep, come)
        come = along(send, reach)
        reach *= 2
    total = call(join_kernel, [part], [VMEM, VMEM], megabytes=4)(keep, come)[0][0]
    return call(
        finish_kernel, jax.ShapeDtypeStruct((rows, width), BF16), [VMEM] * 3, megabytes=8
    )(total, across(total, 1), column)


def solution(mesh):
    in_specs = (
        P("pair", "vir"),
        P(None, ("pair", "vir"), None, None),
        P(None, ("pair", "vir"), None),
        P("pair"),
    )
    out_specs = P("pair", "vir")
    return jax.shard_map(local, mesh=mesh, in_specs=in_specs, out_specs=out_specs, check_vma=False)
```

```python
import functools

import jax
import jax.numpy as jnp
from jax import lax
from jax.experimental import pallas as pl
from jax.experimental.pallas import tpu as pltpu
from jax.sharding import PartitionSpec as P

TILE = 128
SUB = 8
EXTRA = 16
F32 = jnp.float32
BF16 = jnp.bfloat16
VMEM = pl.BlockSpec(memory_space=pltpu.VMEM)
SMEM = pl.BlockSpec(memory_space=pltpu.SMEM)


def call(body, out_shape, in_specs, scratch=(), megabytes=32, aliases=None, out_specs=None):
    many = isinstance(out_shape, (list, tuple))
    return pl.pallas_call(
        body,
        out_shape=out_shape,
        in_specs=in_specs,
        out_specs=out_specs or ([VMEM] * len(out_shape) if many else VMEM),
        scratch_shapes=list(scratch),
        compiler_params=pltpu.CompilerParams(vmem_limit_bytes=megabytes << 20),
        input_output_aliases=aliases or {},
        cost_estimate=pl.CostEstimate(flops=0, bytes_accessed=0, transcendentals=0),
    )


def iota(shape, dimension):
    return lax.broadcasted_iota(jnp.int32, shape, dimension)


def swap_matrix():
    target = iota((TILE, TILE), 1)
    h, a, b = target // (SUB * SUB), target // SUB % SUB, target % SUB
    return iota((TILE, TILE), 0) == (1 - h) * SUB * SUB + b * SUB + a


def cut_kernel(slabs, x_ref, y_ref, *refs):
    for s, out_ref in enumerate(refs[-slabs:]):
        out_ref[...] = (x_ref if s % 2 == 0 else y_ref)[s]


def add_products(grid_ref, acc_refs, tiles_ref, blocks_ref):
    empty = jnp.zeros((TILE, TILE), BF16)
    rows = acc_refs[0].shape[1]

    @pl.loop(0, blocks_ref.shape[1] // 2, unroll=4)
    def _(t):
        to, come = [[blocks_ref[which, 2 * t + k] for k in range(2)] for which in range(2)]
        tiles = [tiles_ref[pl.ds(pl.multiple_of((2 * t + k) * TILE, TILE), TILE), :] for k in range(2)]
        right = jnp.concatenate(
            [jnp.concatenate([tiles[0], empty], axis=1), jnp.concatenate([empty, tiles[1]], axis=1)], axis=0
        )
        products = []
        for side in range(2):
            part = slice(side * rows, (side + 1) * rows)
            left = jnp.concatenate([grid_ref[come[0], part], grid_ref[come[1], part]], axis=1)
            products.append(jnp.dot(left, right, preferred_element_type=F32))
        for k in range(2):
            for side in range(2):
                acc_refs[side][to[k]] += products[side][:, k * TILE : (k + 1) * TILE]


def first_kernel(n_vir, n_sets, *refs):
    own, other = refs[:n_vir], refs[n_vir : 2 * n_vir]
    tiles = refs[2 * n_vir : 2 * n_vir + n_sets]
    blocks = refs[2 * n_vir + n_sets : 2 * n_vir + 2 * n_sets]
    row_ref, grid_ref, *acc_refs = refs[2 * n_vir + 2 * n_sets :]
    rows, width = own[0].shape
    per = width // TILE
    pair = lax.axis_index("pair")
    vir = lax.axis_index("vir")
    upper = pair % 2 == 1
    mirrors = (row_ref[...] - (pair ^ 1) * rows == iota((rows, rows), 0)).astype(F32)
    hot = jnp.where(upper, mirrors, mirrors.T).astype(BF16)
    for shift in range(n_vir):
        first = (vir ^ shift) * per
        mine, others = own[shift][...], other[shift][...]
        kept = jnp.where(upper, others, mine)
        moved = jnp.dot(hot, jnp.where(upper, mine, others), preferred_element_type=F32).astype(BF16)
        for k in range(per):
            columns = slice(k * TILE, (k + 1) * TILE)
            grid_ref[first + k, :rows] = kept[:, columns]
            grid_ref[first + k, rows:] = moved[:, columns]
    for acc_ref in acc_refs:
        acc_ref[...] = jnp.zeros_like(acc_ref)
    for tiles_ref, blocks_ref in zip(tiles, blocks):
        for s in range(tiles_ref.shape[0]):
            add_products(grid_ref, acc_refs, tiles_ref.at[s], blocks_ref.at[s])


def second_kernel(n_vir, n_sets, *refs):
    grid_ref = refs[0]
    tiles, blocks = refs[3 : 3 + n_sets], refs[3 + n_sets : 3 + 2 * n_sets]
    keep_ref, send_ref, *acc_refs = refs[3 + 2 * n_sets :]
    half, rows = keep_ref.shape[1:3]
    core = lax.axis_index("pair") % 2
    vir = lax.axis_index("vir")
    for tiles_ref, blocks_ref in zip(tiles, blocks):
        for s in range(tiles_ref.shape[0]):
            add_products(grid_ref, acc_refs, tiles_ref.at[s], blocks_ref.at[s])
    swap = swap_matrix().astype(BF16)
    for shift in range(n_vir):
        for k in range(half):
            for out_ref, side in ((keep_ref, core), (send_ref, 1 - core)):
                block = ((vir ^ shift) * 2 + side) * half + k
                upper = acc_refs[1][block].astype(BF16)
                total = acc_refs[0][block] + jnp.dot(upper, swap, preferred_element_type=F32)
                out_ref[shift, k] = total.astype(BF16)


def join_kernel(keep_ref, come_ref, *outs):
    for shift, out_ref in enumerate(outs):
        out_ref[...] = (keep_ref[shift].astype(F32) + come_ref[shift].astype(F32)).astype(BF16)


def total_kernel(*refs):
    total = refs[0][...].astype(F32)
    for ref in refs[1:-1]:
        total += ref[...].astype(F32)
    refs[-1][...] = total.astype(BF16)


def finish_kernel(own_ref, other_ref, row_ref, out_ref):
    half, rows, _ = own_ref.shape
    pair = lax.axis_index("pair")
    upper = pair % 2 == 1
    place = jnp.where(upper, row_ref[...] - (pair ^ 1) * rows, iota((1, rows), 1))
    hot = (iota((rows, rows), 0) == place).astype(F32).T.astype(BF16)
    same = (iota((TILE, TILE), 0) == iota((TILE, TILE), 1)).astype(F32)
    swap = jnp.where(upper, swap_matrix().astype(F32), same).astype(BF16)
    for which in range(2):
        for k in range(half):
            values = jnp.where(upper == (which == 1), own_ref[k], other_ref[k])
            values = jnp.dot(values, swap, preferred_element_type=F32).astype(BF16)
            column = (which * half + k) * TILE
            out_ref[:, column : column + TILE] = jnp.dot(hot, values, preferred_element_type=F32).astype(BF16)


def local(amplitudes, integrals, tile_blocks, mirror_row):
    rows, width = amplitudes.shape
    slabs, tile_dev = integrals.shape[:2]
    n_pair, n_vir = lax.axis_size("pair"), lax.axis_size("vir")
    chips = n_pair // 2
    per = width // TILE
    n_blk = per * n_vir
    length = tile_dev * TILE

    def across(array, bits):
        return lax.ppermute(array, "pair", [(i, i ^ bits) for i in range(n_pair)])

    def along(array, bits):
        return lax.ppermute(array, "vir", [(i, i ^ bits) for i in range(n_vir)])

    ids = tile_blocks.transpose(0, 2, 1).astype(BF16)
    ids = jnp.pad(ids, ((0, 0), (0, EXTRA - 2), (0, TILE - tile_dev)))
    packed = jnp.concatenate([integrals.reshape(slabs, length, TILE), ids], axis=1)
    early = [packed, across(packed, 2), across(packed, 4)]

    pieces = {0: amplitudes}
    reach = n_vir // 2
    while reach:
        pieces |= {shift + reach: along(piece, reach) for shift, piece in pieces.items()}
        reach //= 2
    mine = [pieces[shift] for shift in range(n_vir)]
    others = [across(piece, 1) for piece in mine]
    first = [*others[:-1], *mine[1:-1]]
    slab = jax.ShapeDtypeStruct((length + EXTRA, TILE), BF16)
    halves = call(
        functools.partial(cut_kernel, slabs),
        [slab] * slabs,
        [VMEM, VMEM] + [pl.BlockSpec(memory_space=pl.ANY)] * len(first),
        megabytes=4,
    )(early[1], early[2], *first)
    late = [across(half, 4 if s % 2 == 0 else 2) for s, half in enumerate(halves)]
    reach = 4
    while reach < chips:
        farther = early + late if reach == 4 else late
        late = late + [across(array, 2 * reach) for array in farther]
        reach *= 2
    late = [array.reshape(-1, length + EXTRA, TILE) for array in late]
    row = mirror_row.reshape(1, rows)

    def ids(array):
        return array[:, length : length + 2, :tile_dev].astype(jnp.int32)

    sums = jax.ShapeDtypeStruct((n_blk, rows, TILE), F32)
    grid, *sums_so_far = call(
        functools.partial(first_kernel, n_vir, len(early)),
        [jax.ShapeDtypeStruct((n_blk, 2 * rows, TILE), BF16), sums, sums],
        [VMEM] * (2 * n_vir + len(early)) + [SMEM] * len(early) + [VMEM],
        megabytes=20,
    )(*mine, *others, *early, *[ids(array) for array in early], row)
    piece = jax.ShapeDtypeStruct((n_vir, per // 2, rows, TILE), BF16)
    keep, send, *_ = call(
        functools.partial(second_kernel, n_vir, len(late)),
        [piece, piece, sums, sums],
        [VMEM] * (3 + len(late)) + [SMEM] * len(late),
        megabytes=24,
        aliases={1: 2, 2: 3},
    )(grid, *sums_so_far, *late, *[ids(array) for array in late])
    one = jax.ShapeDtypeStruct((per // 2, rows, TILE), BF16)
    parts = call(join_kernel, [one] * n_vir, [VMEM, VMEM], megabytes=4)(keep, across(send, 1))
    arrived = [along(parts[shift], shift) for shift in range(n_vir - 1, 0, -1)]
    total = call(total_kernel, one, [VMEM] * n_vir, megabytes=4)(parts[0], *arrived)
    return call(
        finish_kernel, jax.ShapeDtypeStruct((rows, width), BF16), [VMEM] * 3, megabytes=8
    )(total, across(total, 1), row)


def solution(mesh):
    in_specs = (
        P("pair", "vir"),
        P(None, ("pair", "vir"), None, None),
        P(None, ("pair", "vir"), None),
        P("pair"),
    )
    out_specs = P("pair", "vir")
    return jax.shard_map(local, mesh=mesh, in_specs=in_specs, out_specs=out_specs, check_vma=False)
```

```python
import functools

import jax
import jax.numpy as jnp
from jax import lax
from jax.experimental import pallas as pl
from jax.experimental.pallas import tpu as pltpu
from jax.sharding import PartitionSpec as P

TILE = 128
SUB = 8
EXTRA = 16
F32 = jnp.float32
BF16 = jnp.bfloat16
VMEM = pl.BlockSpec(memory_space=pltpu.VMEM)
SMEM = pl.BlockSpec(memory_space=pltpu.SMEM)


def call(body, out_shape, in_specs, scratch=(), megabytes=32, aliases=None, flops=0, moved=0):
    many = isinstance(out_shape, (list, tuple))
    return pl.pallas_call(
        body,
        out_shape=out_shape,
        in_specs=in_specs,
        out_specs=[VMEM] * len(out_shape) if many else VMEM,
        scratch_shapes=list(scratch),
        compiler_params=pltpu.CompilerParams(vmem_limit_bytes=megabytes << 20),
        input_output_aliases=aliases or {},
        cost_estimate=pl.CostEstimate(flops=flops, bytes_accessed=moved, transcendentals=0),
    )


def iota(shape, dimension):
    return lax.broadcasted_iota(jnp.int32, shape, dimension)


def swap_matrix():
    target = iota((TILE, TILE), 1)
    h, a, b = target // (SUB * SUB), target // SUB % SUB, target % SUB
    return iota((TILE, TILE), 0) == (1 - h) * SUB * SUB + b * SUB + a


def cut_kernel(slabs, x_ref, y_ref, *refs):
    for s, out_ref in enumerate(refs[-slabs:]):
        out_ref[...] = (x_ref if s % 2 == 0 else y_ref)[s]


def add_products(grid_ref, acc_refs, tiles_ref, blocks_ref):
    empty = jnp.zeros((TILE, TILE), BF16)
    rows = acc_refs[0].shape[1]

    @pl.loop(0, blocks_ref.shape[1] // 2, unroll=4)
    def _(t):
        to, come = [[blocks_ref[which, 2 * t + k] for k in range(2)] for which in range(2)]
        tiles = [tiles_ref[pl.ds(pl.multiple_of((2 * t + k) * TILE, TILE), TILE), :] for k in range(2)]
        right = jnp.concatenate(
            [jnp.concatenate([tiles[0], empty], axis=1), jnp.concatenate([empty, tiles[1]], axis=1)], axis=0
        )
        products = []
        for side in range(2):
            part = slice(side * rows, (side + 1) * rows)
            left = jnp.concatenate([grid_ref[come[0], part], grid_ref[come[1], part]], axis=1)
            products.append(jnp.dot(left, right, preferred_element_type=F32))
        for k in range(2):
            for side in range(2):
                acc_refs[side][to[k]] += products[side][:, k * TILE : (k + 1) * TILE]


def first_kernel(n_vir, n_sets, *refs):
    own, other = refs[:n_vir], refs[n_vir : 2 * n_vir]
    tiles = refs[2 * n_vir : 2 * n_vir + n_sets]
    blocks = refs[2 * n_vir + n_sets : 2 * n_vir + 2 * n_sets]
    row_ref, grid_ref, *acc_refs = refs[2 * n_vir + 2 * n_sets :]
    rows, width = own[0].shape
    per = width // TILE
    pair = lax.axis_index("pair")
    vir = lax.axis_index("vir")
    upper = pair % 2 == 1
    mirrors = (row_ref[...] - (pair ^ 1) * rows == iota((rows, rows), 0)).astype(F32)
    hot = jnp.where(upper, mirrors, mirrors.T).astype(BF16)
    for shift in range(n_vir):
        first = (vir ^ shift) * per
        mine, others = own[shift][...], other[shift][...]
        kept = jnp.where(upper, others, mine)
        moved = jnp.dot(hot, jnp.where(upper, mine, others), preferred_element_type=F32).astype(BF16)
        for k in range(per):
            columns = slice(k * TILE, (k + 1) * TILE)
            grid_ref[first + k, :rows] = kept[:, columns]
            grid_ref[first + k, rows:] = moved[:, columns]
    for acc_ref in acc_refs:
        acc_ref[...] = jnp.zeros_like(acc_ref)
    for tiles_ref, blocks_ref in zip(tiles, blocks):
        for s in range(tiles_ref.shape[0]):
            add_products(grid_ref, acc_refs, tiles_ref.at[s], blocks_ref.at[s])


def more_kernel(n_sets, *refs):
    grid_ref = refs[0]
    tiles, blocks = refs[3 : 3 + n_sets], refs[3 + n_sets : 3 + 2 * n_sets]
    acc_refs = refs[3 + 2 * n_sets :]
    for tiles_ref, blocks_ref in zip(tiles, blocks):
        for s in range(tiles_ref.shape[0]):
            add_products(grid_ref, acc_refs, tiles_ref.at[s], blocks_ref.at[s])


def last_kernel(n_vir, n_sets, *refs):
    keep_ref, send_ref, *acc_refs = refs[3 + 2 * n_sets :]
    more_kernel(n_sets, *refs[: 3 + 2 * n_sets], *acc_refs)
    half = keep_ref.shape[1]
    core = lax.axis_index("pair") % 2
    vir = lax.axis_index("vir")
    swap = swap_matrix().astype(BF16)
    for shift in range(n_vir):
        for k in range(half):
            for out_ref, side in ((keep_ref, core), (send_ref, 1 - core)):
                block = ((vir ^ shift) * 2 + side) * half + k
                upper = acc_refs[1][block].astype(BF16)
                total = acc_refs[0][block] + jnp.dot(upper, swap, preferred_element_type=F32)
                out_ref[shift, k] = total.astype(BF16)


def join_kernel(keep_ref, come_ref, *outs):
    for shift, out_ref in enumerate(outs):
        out_ref[...] = (keep_ref[shift].astype(F32) + come_ref[shift].astype(F32)).astype(BF16)


def total_kernel(*refs):
    total = refs[0][...].astype(F32)
    for ref in refs[1:-1]:
        total += ref[...].astype(F32)
    refs[-1][...] = total.astype(BF16)


def finish_kernel(own_ref, other_ref, row_ref, out_ref):
    half, rows, _ = own_ref.shape
    pair = lax.axis_index("pair")
    upper = pair % 2 == 1
    place = jnp.where(upper, row_ref[...] - (pair ^ 1) * rows, iota((1, rows), 1))
    hot = (iota((rows, rows), 0) == place).astype(F32).T.astype(BF16)
    same = (iota((TILE, TILE), 0) == iota((TILE, TILE), 1)).astype(F32)
    swap = jnp.where(upper, swap_matrix().astype(F32), same).astype(BF16)
    for which in range(2):
        for k in range(half):
            values = jnp.where(upper == (which == 1), own_ref[k], other_ref[k])
            values = jnp.dot(values, swap, preferred_element_type=F32).astype(BF16)
            column = (which * half + k) * TILE
            out_ref[:, column : column + TILE] = jnp.dot(hot, values, preferred_element_type=F32).astype(BF16)


def local(amplitudes, integrals, tile_blocks, mirror_row):
    rows, width = amplitudes.shape
    slabs, tile_dev = integrals.shape[:2]
    n_pair, n_vir = lax.axis_size("pair"), lax.axis_size("vir")
    chips = n_pair // 2
    per = width // TILE
    n_blk = per * n_vir
    length = tile_dev * TILE

    def across(array, bits):
        return lax.ppermute(array, "pair", [(i, i ^ bits) for i in range(n_pair)])

    def along(array, bits):
        return lax.ppermute(array, "vir", [(i, i ^ bits) for i in range(n_vir)])

    ids = tile_blocks.transpose(0, 2, 1).reshape(1, 2 * slabs, tile_dev).astype(BF16)
    ids = jnp.pad(ids, ((0, 0), (0, EXTRA - 2 * slabs), (0, TILE - tile_dev)))
    ids = jnp.broadcast_to(ids, (slabs, EXTRA, TILE))
    packed = jnp.concatenate([integrals.reshape(slabs, length, TILE), ids], axis=1)
    early = [packed, across(packed, 2), across(packed, 4)]

    pieces = {0: amplitudes}
    reach = n_vir // 2
    while reach:
        pieces |= {shift + reach: along(piece, reach) for shift, piece in pieces.items()}
        reach //= 2
    mine = [pieces[shift] for shift in range(n_vir)]
    others = [across(piece, 1) for piece in mine]
    first = [*others, *mine[1:]]
    slab = jax.ShapeDtypeStruct((length + EXTRA, TILE), BF16)
    halves = call(
        functools.partial(cut_kernel, slabs),
        [slab] * slabs,
        [VMEM, VMEM] + [pl.BlockSpec(memory_space=pl.ANY)] * len(first),
        megabytes=4,
    )(early[1], early[2], *first)
    late = [across(half, 4 if s % 2 == 0 else 2) for s, half in enumerate(halves)]
    reach = 4
    while reach < chips:
        farther = early + late if reach == 4 else late
        late = late + [across(array, 2 * reach) for array in farther]
        reach *= 2
    late = [array.reshape(-1, length + EXTRA, TILE) for array in late]
    row = mirror_row.reshape(1, rows)

    def ids_in(array):
        return array[0, length : length + 2 * slabs, :tile_dev].astype(jnp.int32).reshape(slabs, 2, tile_dev)

    diagonal = ids_in(late[0])
    late_ids = [diagonal[s : s + 1] for s in range(slabs)] + [ids_in(array) for array in late[slabs:]]
    sums = jax.ShapeDtypeStruct((n_blk, rows, TILE), F32)
    grid, *sums_so_far = call(
        functools.partial(first_kernel, n_vir, len(early)),
        [jax.ShapeDtypeStruct((n_blk, 2 * rows, TILE), BF16), sums, sums],
        [VMEM] * (2 * n_vir + len(early)) + [SMEM] * len(early) + [VMEM],
        megabytes=20,
    )(*mine, *others, *early, *[ids_in(array) for array in early], row)
    sums_so_far = call(
        functools.partial(more_kernel, 1),
        [sums, sums],
        [VMEM] * 4 + [SMEM],
        megabytes=20,
        aliases={1: 0, 2: 1},
        flops=2 * tile_dev * 2 * rows * 2 * TILE * TILE,
        moved=8 << 20,
    )(grid, *sums_so_far, late[0], late_ids[0])
    piece = jax.ShapeDtypeStruct((n_vir, per // 2, rows, TILE), BF16)
    keep, send, *_ = call(
        functools.partial(last_kernel, n_vir, len(late) - 1),
        [piece, piece, sums, sums],
        [VMEM] * (2 + len(late)) + [SMEM] * (len(late) - 1),
        megabytes=24,
        aliases={1: 2, 2: 3},
    )(grid, *sums_so_far, *late[1:], *late_ids[1:])
    one = jax.ShapeDtypeStruct((per // 2, rows, TILE), BF16)
    parts = call(join_kernel, [one] * n_vir, [VMEM, VMEM], megabytes=4)(keep, across(send, 1))
    arrived = [along(parts[shift], shift) for shift in range(n_vir - 1, 0, -1)]
    total = call(total_kernel, one, [VMEM] * n_vir, megabytes=4)(parts[0], *arrived)
    return call(
        finish_kernel, jax.ShapeDtypeStruct((rows, width), BF16), [VMEM] * 3, megabytes=8
    )(total, across(total, 1), row)


def solution(mesh):
    in_specs = (
        P("pair", "vir"),
        P(None, ("pair", "vir"), None, None),
        P(None, ("pair", "vir"), None),
        P("pair"),
    )
    out_specs = P("pair", "vir")
    return jax.shard_map(local, mesh=mesh, in_specs=in_specs, out_specs=out_specs, check_vma=False)
```

```python
import functools

import jax
import jax.numpy as jnp
from jax import lax
from jax.experimental import pallas as pl
from jax.experimental.pallas import tpu as pltpu
from jax.sharding import PartitionSpec as P

TILE = 128
SUB = 8
EXTRA = 16
F32 = jnp.float32
BF16 = jnp.bfloat16
VMEM = pl.BlockSpec(memory_space=pltpu.VMEM)
SMEM = pl.BlockSpec(memory_space=pltpu.SMEM)


def call(body, out_shape, in_specs, scratch=(), megabytes=32, aliases=None):
    many = isinstance(out_shape, (list, tuple))
    return pl.pallas_call(
        body,
        out_shape=out_shape,
        in_specs=in_specs,
        out_specs=[VMEM] * len(out_shape) if many else VMEM,
        scratch_shapes=list(scratch),
        compiler_params=pltpu.CompilerParams(vmem_limit_bytes=megabytes << 20),
        input_output_aliases=aliases or {},
        cost_estimate=pl.CostEstimate(flops=0, bytes_accessed=0, transcendentals=0),
    )


def iota(shape, dimension):
    return lax.broadcasted_iota(jnp.int32, shape, dimension)


def swap_matrix():
    target = iota((TILE, TILE), 1)
    h, a, b = target // (SUB * SUB), target // SUB % SUB, target % SUB
    return iota((TILE, TILE), 0) == (1 - h) * SUB * SUB + b * SUB + a


def cut_kernel(slabs, x_ref, y_ref, *refs):
    for s, out_ref in enumerate(refs[-slabs:]):
        out_ref[...] = (x_ref if s % 2 == 0 else y_ref)[s]


def add_products(grid_ref, acc_refs, tiles_ref, blocks_ref):
    empty = jnp.zeros((TILE, TILE), BF16)
    rows = acc_refs[0].shape[1]

    @pl.loop(0, blocks_ref.shape[1] // 2, unroll=4)
    def _(t):
        to, come = [[blocks_ref[which, 2 * t + k] for k in range(2)] for which in range(2)]
        tiles = [tiles_ref[pl.ds(pl.multiple_of((2 * t + k) * TILE, TILE), TILE), :] for k in range(2)]
        right = jnp.concatenate(
            [jnp.concatenate([tiles[0], empty], axis=1), jnp.concatenate([empty, tiles[1]], axis=1)], axis=0
        )
        products = []
        for side in range(2):
            part = slice(side * rows, (side + 1) * rows)
            left = jnp.concatenate([grid_ref[come[0], part], grid_ref[come[1], part]], axis=1)
            products.append(jnp.dot(left, right, preferred_element_type=F32))
        for k in range(2):
            for side in range(2):
                acc_refs[side][to[k]] += products[side][:, k * TILE : (k + 1) * TILE]


def first_kernel(n_vir, n_sets, *refs):
    own, other = refs[:n_vir], refs[n_vir : 2 * n_vir]
    tiles = refs[2 * n_vir : 2 * n_vir + n_sets]
    blocks = refs[2 * n_vir + n_sets : 2 * n_vir + 2 * n_sets]
    row_ref, grid_ref, last_hot_ref, *acc_refs = refs[2 * n_vir + 2 * n_sets :]
    rows, width = own[0].shape
    per = width // TILE
    pair = lax.axis_index("pair")
    vir = lax.axis_index("vir")
    upper = pair % 2 == 1
    mirrors = (row_ref[...] - (pair ^ 1) * rows == iota((rows, rows), 0)).astype(F32)
    turned = mirrors.T
    hot = jnp.where(upper, mirrors, turned).astype(BF16)
    same = (iota((rows, rows), 0) == iota((rows, rows), 1)).astype(F32)
    last_hot_ref[...] = jnp.where(upper, turned, same).astype(BF16)
    for shift in range(n_vir):
        first = (vir ^ shift) * per
        mine, others = own[shift][...], other[shift][...]
        kept = jnp.where(upper, others, mine)
        moved = jnp.dot(hot, jnp.where(upper, mine, others), preferred_element_type=F32).astype(BF16)
        for k in range(per):
            columns = slice(k * TILE, (k + 1) * TILE)
            grid_ref[first + k, :rows] = kept[:, columns]
            grid_ref[first + k, rows:] = moved[:, columns]
    for acc_ref in acc_refs:
        acc_ref[...] = jnp.zeros_like(acc_ref)
    for tiles_ref, blocks_ref in zip(tiles, blocks):
        for s in range(tiles_ref.shape[0]):
            add_products(grid_ref, acc_refs, tiles_ref.at[s], blocks_ref.at[s])


def more_kernel(n_sets, *refs):
    grid_ref = refs[0]
    tiles, blocks = refs[3 : 3 + n_sets], refs[3 + n_sets : 3 + 2 * n_sets]
    acc_refs = refs[3 + 2 * n_sets :]
    for tiles_ref, blocks_ref in zip(tiles, blocks):
        for s in range(tiles_ref.shape[0]):
            add_products(grid_ref, acc_refs, tiles_ref.at[s], blocks_ref.at[s])


def fold_kernel(shifts, own_ref, mirror_ref, keep_ref, send_ref):
    half = keep_ref.shape[1]
    core = lax.axis_index("pair") % 2
    vir = lax.axis_index("vir")
    swap = swap_matrix().astype(BF16)
    for place, shift in enumerate(shifts):
        for k in range(half):
            for out_ref, side in ((keep_ref, core), (send_ref, 1 - core)):
                block = ((vir ^ shift) * 2 + side) * half + k
                upper = mirror_ref[block].astype(BF16)
                total = own_ref[block] + jnp.dot(upper, swap, preferred_element_type=F32)
                out_ref[place, k] = total.astype(BF16)


def join_kernel(keep_ref, come_ref, *outs):
    for shift, out_ref in enumerate(outs):
        out_ref[...] = (keep_ref[shift].astype(F32) + come_ref[shift].astype(F32)).astype(BF16)


def total_kernel(*refs):
    total = refs[0][...].astype(F32)
    for ref in refs[1:-1]:
        total += ref[...].astype(F32)
    refs[-1][...] = total.astype(BF16)


def finish_kernel(own_ref, other_ref, hot_ref, out_ref):
    half = own_ref.shape[0]
    upper = lax.axis_index("pair") % 2 == 1
    hot = hot_ref[...]
    same = (iota((TILE, TILE), 0) == iota((TILE, TILE), 1)).astype(F32)
    swap = jnp.where(upper, swap_matrix().astype(F32), same).astype(BF16)
    for which in range(2):
        for k in range(half):
            values = jnp.where(upper == (which == 1), own_ref[k], other_ref[k])
            values = jnp.dot(values, swap, preferred_element_type=F32).astype(BF16)
            column = (which * half + k) * TILE
            out_ref[:, column : column + TILE] = jnp.dot(hot, values, preferred_element_type=F32).astype(BF16)


def local(amplitudes, integrals, tile_blocks, mirror_row):
    rows, width = amplitudes.shape
    slabs, tile_dev = integrals.shape[:2]
    n_pair, n_vir = lax.axis_size("pair"), lax.axis_size("vir")
    chips = n_pair // 2
    per = width // TILE
    n_blk = per * n_vir
    length = tile_dev * TILE

    def across(array, bits):
        return lax.ppermute(array, "pair", [(i, i ^ bits) for i in range(n_pair)])

    def along(array, bits):
        return lax.ppermute(array, "vir", [(i, i ^ bits) for i in range(n_vir)])

    ids = tile_blocks.transpose(0, 2, 1).reshape(1, 2 * slabs, tile_dev).astype(BF16)
    ids = jnp.pad(ids, ((0, 0), (0, EXTRA - 2 * slabs), (0, TILE - tile_dev)))
    ids = jnp.broadcast_to(ids, (slabs, EXTRA, TILE))
    packed = jnp.concatenate([integrals.reshape(slabs, length, TILE), ids], axis=1)
    early = [packed, across(packed, 2), across(packed, 4)]

    pieces = {0: amplitudes}
    reach = n_vir // 2
    while reach:
        pieces |= {shift + reach: along(piece, reach) for shift, piece in pieces.items()}
        reach //= 2
    mine = [pieces[shift] for shift in range(n_vir)]
    others = [across(piece, 1) for piece in mine]
    first = [*others, *mine[1:]]
    slab = jax.ShapeDtypeStruct((length + EXTRA, TILE), BF16)
    halves = call(
        functools.partial(cut_kernel, slabs),
        [slab] * slabs,
        [VMEM, VMEM] + [pl.BlockSpec(memory_space=pl.ANY)] * len(first),
        megabytes=4,
    )(early[1], early[2], *first)
    late = [across(half, 4 if s % 2 == 0 else 2) for s, half in enumerate(halves)]
    reach = 4
    while reach < chips:
        farther = early + late if reach == 4 else late
        late = late + [across(array, 2 * reach) for array in farther]
        reach *= 2
    late = [array.reshape(-1, length + EXTRA, TILE) for array in late]
    row = mirror_row.reshape(1, rows)

    def ids_in(array):
        return array[0, length : length + 2 * slabs, :tile_dev].astype(jnp.int32).reshape(slabs, 2, tile_dev)

    diagonal = ids_in(late[0])
    late_ids = [diagonal[s : s + 1] for s in range(slabs)] + [ids_in(array) for array in late[slabs:]]
    sums = jax.ShapeDtypeStruct((n_blk, rows, TILE), F32)
    grid, last_hot, *sums_so_far = call(
        functools.partial(first_kernel, n_vir, len(early)),
        [
            jax.ShapeDtypeStruct((n_blk, 2 * rows, TILE), BF16),
            jax.ShapeDtypeStruct((rows, rows), BF16),
            sums,
            sums,
        ],
        [VMEM] * (2 * n_vir + len(early)) + [SMEM] * len(early) + [VMEM],
        megabytes=20,
    )(*mine, *others, *early, *[ids_in(array) for array in early], row)
    sums_so_far = call(
        functools.partial(more_kernel, len(late)),
        [sums, sums],
        [VMEM] * (3 + len(late)) + [SMEM] * len(late),
        megabytes=24,
        aliases={1: 0, 2: 1},
    )(grid, *sums_so_far, *late, *late_ids)

    parts = {}
    for shifts in (range(n_vir - 1, n_vir // 2 - 1, -1), range(n_vir // 2 - 1, -1, -1)):
        piece = jax.ShapeDtypeStruct((len(shifts), per // 2, rows, TILE), BF16)
        keep, send = call(
            functools.partial(fold_kernel, shifts), [piece, piece], [VMEM, VMEM], megabytes=8
        )(*sums_so_far)
        one = jax.ShapeDtypeStruct((per // 2, rows, TILE), BF16)
        joined = call(join_kernel, [one] * len(shifts), [VMEM, VMEM], megabytes=4)(keep, across(send, 1))
        parts |= {shift: along(part, shift) if shift else part for shift, part in zip(shifts, joined)}
    total = call(total_kernel, one, [VMEM] * n_vir, megabytes=4)(*[parts[shift] for shift in range(n_vir)])
    return call(
        finish_kernel, jax.ShapeDtypeStruct((rows, width), BF16), [VMEM] * 3, megabytes=8
    )(total, across(total, 1), last_hot)


def solution(mesh):
    in_specs = (
        P("pair", "vir"),
        P(None, ("pair", "vir"), None, None),
        P(None, ("pair", "vir"), None),
        P("pair"),
    )
    out_specs = P("pair", "vir")
    return jax.shard_map(local, mesh=mesh, in_specs=in_specs, out_specs=out_specs, check_vma=False)
```

```python
import functools

import jax
import jax.numpy as jnp
from jax import lax
from jax.experimental import pallas as pl
from jax.experimental.pallas import tpu as pltpu
from jax.sharding import PartitionSpec as P

TILE = 128
SUB = 8
EXTRA = 16
F32 = jnp.float32
BF16 = jnp.bfloat16
VMEM = pl.BlockSpec(memory_space=pltpu.VMEM)
SMEM = pl.BlockSpec(memory_space=pltpu.SMEM)


def call(body, out_shape, in_specs, scratch=(), megabytes=32, aliases=None, out_specs=None):
    many = isinstance(out_shape, (list, tuple))
    return pl.pallas_call(
        body,
        out_shape=out_shape,
        in_specs=in_specs,
        out_specs=out_specs or ([VMEM] * len(out_shape) if many else VMEM),
        scratch_shapes=list(scratch),
        compiler_params=pltpu.CompilerParams(vmem_limit_bytes=megabytes << 20),
        input_output_aliases=aliases or {},
        cost_estimate=pl.CostEstimate(flops=0, bytes_accessed=0, transcendentals=0),
    )


def iota(shape, dimension):
    return lax.broadcasted_iota(jnp.int32, shape, dimension)


def swap_matrix():
    target = iota((TILE, TILE), 1)
    h, a, b = target // (SUB * SUB), target // SUB % SUB, target % SUB
    return iota((TILE, TILE), 0) == (1 - h) * SUB * SUB + b * SUB + a


def cut_kernel(slabs, x_ref, y_ref, *refs):
    for s in range(slabs):
        slab_ref = (x_ref if s % 2 == 0 else y_ref).at[s]
        upper_ref, lower_ref = refs[2 * (s - slabs)], refs[2 * (s - slabs) + 1]
        middle = upper_ref.shape[0]
        upper_ref[...] = slab_ref[:middle]
        lower_ref[...] = slab_ref[middle:]


def add_products(grid_ref, acc_refs, tiles_ref, blocks_ref, first=EXTRA):
    empty = jnp.zeros((TILE, TILE), BF16)
    rows = acc_refs[0].shape[1]

    @pl.loop(0, blocks_ref.shape[1] // 2, unroll=4)
    def _(t):
        to, come = [[blocks_ref[which, 2 * t + k] for k in range(2)] for which in range(2)]
        tiles = [tiles_ref[pl.ds(pl.multiple_of((2 * t + k) * TILE + first, EXTRA), TILE), :] for k in range(2)]
        right = jnp.concatenate(
            [jnp.concatenate([tiles[0], empty], axis=1), jnp.concatenate([empty, tiles[1]], axis=1)], axis=0
        )
        products = []
        for side in range(2):
            part = slice(side * rows, (side + 1) * rows)
            left = jnp.concatenate([grid_ref[come[0], part], grid_ref[come[1], part]], axis=1)
            products.append(jnp.dot(left, right, preferred_element_type=F32))
        for k in range(2):
            for side in range(2):
                acc_refs[side][to[k]] += products[side][:, k * TILE : (k + 1) * TILE]


def first_kernel(n_vir, n_sets, *refs):
    own, other = refs[:n_vir], refs[n_vir : 2 * n_vir]
    tiles = refs[2 * n_vir : 2 * n_vir + n_sets]
    blocks = refs[2 * n_vir + n_sets : 2 * n_vir + 2 * n_sets]
    row_ref, grid_ref, last_hot_ref, *acc_refs = refs[2 * n_vir + 2 * n_sets :]
    rows, width = own[0].shape
    per = width // TILE
    pair = lax.axis_index("pair")
    vir = lax.axis_index("vir")
    upper = pair % 2 == 1
    mirrors = (row_ref[...] - (pair ^ 1) * rows == iota((rows, rows), 0)).astype(F32)
    turned = mirrors.T
    hot = jnp.where(upper, mirrors, turned).astype(BF16)
    same = (iota((rows, rows), 0) == iota((rows, rows), 1)).astype(F32)
    last_hot_ref[...] = jnp.where(upper, turned, same).astype(BF16)
    for shift in range(n_vir):
        first = (vir ^ shift) * per
        mine, others = own[shift][...], other[shift][...]
        kept = jnp.where(upper, others, mine)
        moved = jnp.dot(hot, jnp.where(upper, mine, others), preferred_element_type=F32).astype(BF16)
        for k in range(per):
            columns = slice(k * TILE, (k + 1) * TILE)
            grid_ref[first + k, :rows] = kept[:, columns]
            grid_ref[first + k, rows:] = moved[:, columns]
    for acc_ref in acc_refs:
        acc_ref[...] = jnp.zeros_like(acc_ref)
    for tiles_ref, blocks_ref in zip(tiles, blocks):
        for s in range(tiles_ref.shape[0]):
            add_products(grid_ref, acc_refs, tiles_ref.at[s], blocks_ref.at[s])


def more_kernel(n_sets, *refs):
    grid_ref = refs[0]
    tiles, blocks = refs[3 : 3 + n_sets], refs[3 + n_sets : 3 + 2 * n_sets]
    acc_refs = refs[3 + 2 * n_sets :]
    for tiles_ref, blocks_ref in zip(tiles, blocks):
        for s in range(tiles_ref.shape[0]):
            first = tiles_ref.shape[1] % TILE
            add_products(grid_ref, acc_refs, tiles_ref.at[s], blocks_ref.at[s], first)


def fold_kernel(shifts, own_ref, mirror_ref, keep_ref, send_ref):
    half = keep_ref.shape[1]
    core = lax.axis_index("pair") % 2
    vir = lax.axis_index("vir")
    swap = swap_matrix().astype(BF16)
    for place, shift in enumerate(shifts):
        for k in range(half):
            for out_ref, side in ((keep_ref, core), (send_ref, 1 - core)):
                block = ((vir ^ shift) * 2 + side) * half + k
                upper = mirror_ref[block].astype(BF16)
                total = own_ref[block] + jnp.dot(upper, swap, preferred_element_type=F32)
                out_ref[place, k] = total.astype(BF16)


def join_kernel(keep_ref, come_ref, *outs):
    for shift, out_ref in enumerate(outs):
        out_ref[...] = (keep_ref[shift].astype(F32) + come_ref[shift].astype(F32)).astype(BF16)


def total_kernel(*refs):
    total = refs[0][...].astype(F32)
    for ref in refs[1:-1]:
        total += ref[...].astype(F32)
    refs[-1][...] = total.astype(BF16)


def finish_kernel(own_ref, other_ref, hot_ref, out_ref, made_ref, sems):
    half = own_ref.shape[0]
    upper = lax.axis_index("pair") % 2 == 1
    hot = hot_ref[...]
    same = (iota((TILE, TILE), 0) == iota((TILE, TILE), 1)).astype(F32)
    swap = jnp.where(upper, swap_matrix().astype(F32), same).astype(BF16)
    copies = []
    for which in range(2):
        for k in range(half):
            values = jnp.where(upper == (which == 1), own_ref[k], other_ref[k])
            values = jnp.dot(values, swap, preferred_element_type=F32).astype(BF16)
            block = which * half + k
            columns = pl.ds(block * TILE, TILE)
            made_ref[:, columns] = jnp.dot(hot, values, preferred_element_type=F32).astype(BF16)
            copies.append(pltpu.make_async_copy(made_ref.at[:, columns], out_ref.at[:, columns], sems.at[block]))
            copies[-1].start()
    for copy in copies:
        copy.wait()


def local(amplitudes, integrals, tile_blocks, mirror_row):
    rows, width = amplitudes.shape
    slabs, tile_dev = integrals.shape[:2]
    n_pair, n_vir = lax.axis_size("pair"), lax.axis_size("vir")
    chips = n_pair // 2
    per = width // TILE
    n_blk = per * n_vir
    length = tile_dev * TILE

    def across(array, bits):
        return lax.ppermute(array, "pair", [(i, i ^ bits) for i in range(n_pair)])

    def along(array, bits):
        return lax.ppermute(array, "vir", [(i, i ^ bits) for i in range(n_vir)])

    ids = tile_blocks.transpose(0, 2, 1).reshape(1, 2 * slabs, tile_dev).astype(BF16)
    ids = jnp.pad(ids, ((0, 0), (0, EXTRA - 2 * slabs), (0, TILE - tile_dev)))
    ids = jnp.broadcast_to(ids, (slabs, EXTRA, TILE))
    packed = jnp.concatenate([ids, integrals.reshape(slabs, length, TILE)], axis=1)
    early = [packed, across(packed, 2), across(packed, 4)]

    pieces = {0: amplitudes}
    reach = n_vir // 2
    while reach:
        pieces |= {shift + reach: along(piece, reach) for shift, piece in pieces.items()}
        reach //= 2
    mine = [pieces[shift] for shift in range(n_vir)]
    others = [across(piece, 1) for piece in mine]
    first = [*others, *mine[1:]]
    middle = EXTRA + length // 2
    halves = call(
        functools.partial(cut_kernel, slabs),
        [jax.ShapeDtypeStruct((size, TILE), BF16) for _ in range(slabs) for size in (middle, length // 2)],
        [VMEM, VMEM] + [pl.BlockSpec(memory_space=pl.ANY)] * len(first),
        megabytes=4,
    )(early[1], early[2], *first)
    late = [[across(half, 4 if s % 2 == 0 else 2) for s, half in enumerate(halves[part::2])] for part in range(2)]
    farther, reach = [], 4
    while reach < chips:
        if reach == 4:
            diagonal = jnp.stack([jnp.concatenate([late[part][s] for part in range(2)]) for s in range(slabs)])
            farther = [across(array, 2 * reach) for array in (*early, diagonal)]
        else:
            farther += [across(array, 2 * reach) for array in (*early, diagonal, *farther)]
        reach *= 2
    row = mirror_row.reshape(1, rows)

    def ids_in(array):
        return array[: 2 * slabs, :tile_dev].astype(jnp.int32).reshape(slabs, 2, tile_dev)

    sums = jax.ShapeDtypeStruct((n_blk, rows, TILE), F32)
    grid, last_hot, *sums_so_far = call(
        functools.partial(first_kernel, n_vir, len(early)),
        [
            jax.ShapeDtypeStruct((n_blk, 2 * rows, TILE), BF16),
            jax.ShapeDtypeStruct((rows, rows), BF16),
            sums,
            sums,
        ],
        [VMEM] * (2 * n_vir + len(early)) + [SMEM] * len(early) + [VMEM],
        megabytes=20,
    )(*mine, *others, *early, *[ids_in(array[0]) for array in early], row)
    diagonal_ids = ids_in(late[0][0]).reshape(slabs, 2, 2, tile_dev // 2)
    for part in range(2):
        more = [half[None] for half in late[part]] + (farther if part else [])
        more_ids = [diagonal_ids[s : s + 1, :, part] for s in range(slabs)]
        more_ids += [ids_in(array[0]) for array in farther] if part else []
        sums_so_far = call(
            functools.partial(more_kernel, len(more)),
            [sums, sums],
            [VMEM] * (3 + len(more)) + [SMEM] * len(more),
            megabytes=24,
            aliases={1: 0, 2: 1},
        )(grid, *sums_so_far, *more, *more_ids)

    parts = {}
    for shifts in (range(n_vir - 1, n_vir // 2 - 1, -1), range(n_vir // 2 - 1, -1, -1)):
        piece = jax.ShapeDtypeStruct((len(shifts), per // 2, rows, TILE), BF16)
        keep, send = call(
            functools.partial(fold_kernel, shifts), [piece, piece], [VMEM, VMEM], megabytes=8
        )(*sums_so_far)
        one = jax.ShapeDtypeStruct((per // 2, rows, TILE), BF16)
        joined = call(join_kernel, [one] * len(shifts), [VMEM, VMEM], megabytes=4)(keep, across(send, 1))
        parts |= {shift: along(part, shift) if shift else part for shift, part in zip(shifts, joined)}
    total = call(total_kernel, one, [VMEM] * n_vir, megabytes=4)(*[parts[shift] for shift in range(n_vir)])
    return call(
        finish_kernel,
        jax.ShapeDtypeStruct((rows, width), BF16),
        [VMEM] * 3,
        [pltpu.VMEM((rows, width), BF16), pltpu.SemaphoreType.DMA((per,))],
        megabytes=8,
        out_specs=pl.BlockSpec(memory_space=pl.ANY),
    )(total, across(total, 1), last_hot)


def solution(mesh):
    in_specs = (
        P("pair", "vir"),
        P(None, ("pair", "vir"), None, None),
        P(None, ("pair", "vir"), None),
        P("pair"),
    )
    out_specs = P("pair", "vir")
    return jax.shard_map(local, mesh=mesh, in_specs=in_specs, out_specs=out_specs, check_vma=False)
```

```python
import functools

import jax
import jax.numpy as jnp
from jax import lax
from jax.experimental import pallas as pl
from jax.experimental.pallas import tpu as pltpu
from jax.sharding import PartitionSpec as P

TILE = 128
SUB = 8
EXTRA = 16
F32 = jnp.float32
BF16 = jnp.bfloat16
VMEM = pl.BlockSpec(memory_space=pltpu.VMEM)
SMEM = pl.BlockSpec(memory_space=pltpu.SMEM)


def call(body, out_shape, in_specs, scratch=(), megabytes=32, aliases=None, out_specs=None):
    many = isinstance(out_shape, (list, tuple))
    return pl.pallas_call(
        body,
        out_shape=out_shape,
        in_specs=in_specs,
        out_specs=out_specs or ([VMEM] * len(out_shape) if many else VMEM),
        scratch_shapes=list(scratch),
        compiler_params=pltpu.CompilerParams(vmem_limit_bytes=megabytes << 20),
        input_output_aliases=aliases or {},
        cost_estimate=pl.CostEstimate(flops=0, bytes_accessed=0, transcendentals=0),
    )


def iota(shape, dimension):
    return lax.broadcasted_iota(jnp.int32, shape, dimension)


def swap_matrix():
    target = iota((TILE, TILE), 1)
    h, a, b = target // (SUB * SUB), target // SUB % SUB, target % SUB
    return iota((TILE, TILE), 0) == (1 - h) * SUB * SUB + b * SUB + a


def cut_kernel(slabs, x_ref, y_ref, *refs):
    for s in range(slabs):
        slab_ref = (x_ref if s % 2 == 0 else y_ref).at[s]
        upper_ref, lower_ref = refs[2 * (s - slabs)], refs[2 * (s - slabs) + 1]
        middle = upper_ref.shape[0]
        upper_ref[...] = slab_ref[:middle]
        lower_ref[...] = slab_ref[middle:]


def add_products(grid_ref, acc_refs, tiles_ref, blocks_ref, first=EXTRA, start=0):
    empty = jnp.zeros((TILE, TILE), BF16)
    rows = acc_refs[0].shape[1]

    @pl.loop(0, tiles_ref.shape[0] // TILE // 2, unroll=4)
    def _(t):
        to, come = [[blocks_ref[which, start + 2 * t + k] for k in range(2)] for which in range(2)]
        tiles = [tiles_ref[pl.ds(pl.multiple_of((2 * t + k) * TILE + first, EXTRA), TILE), :] for k in range(2)]
        right = jnp.concatenate(
            [jnp.concatenate([tiles[0], empty], axis=1), jnp.concatenate([empty, tiles[1]], axis=1)], axis=0
        )
        products = []
        for side in range(2):
            part = slice(side * rows, (side + 1) * rows)
            left = jnp.concatenate([grid_ref[come[0], part], grid_ref[come[1], part]], axis=1)
            products.append(jnp.dot(left, right, preferred_element_type=F32))
        for k in range(2):
            for side in range(2):
                acc_refs[side][to[k]] += products[side][:, k * TILE : (k + 1) * TILE]


def first_kernel(n_vir, n_sets, *refs):
    own, other = refs[:n_vir], refs[n_vir : 2 * n_vir]
    tiles = refs[2 * n_vir : 2 * n_vir + n_sets]
    blocks = refs[2 * n_vir + n_sets : 2 * n_vir + 2 * n_sets]
    row_ref, grid_ref, last_hot_ref, *acc_refs = refs[2 * n_vir + 2 * n_sets :]
    rows, width = own[0].shape
    per = width // TILE
    pair = lax.axis_index("pair")
    vir = lax.axis_index("vir")
    upper = pair % 2 == 1
    mirrors = (row_ref[...] - (pair ^ 1) * rows == iota((rows, rows), 0)).astype(F32)
    turned = mirrors.T
    hot = jnp.where(upper, mirrors, turned).astype(BF16)
    same = (iota((rows, rows), 0) == iota((rows, rows), 1)).astype(F32)
    last_hot_ref[...] = jnp.where(upper, turned, same).astype(BF16)
    for shift in range(n_vir):
        first = (vir ^ shift) * per
        mine, others = own[shift][...], other[shift][...]
        kept = jnp.where(upper, others, mine)
        moved = jnp.dot(hot, jnp.where(upper, mine, others), preferred_element_type=F32).astype(BF16)
        for k in range(per):
            columns = slice(k * TILE, (k + 1) * TILE)
            grid_ref[first + k, :rows] = kept[:, columns]
            grid_ref[first + k, rows:] = moved[:, columns]
    for acc_ref in acc_refs:
        acc_ref[...] = jnp.zeros_like(acc_ref)
    for tiles_ref, blocks_ref in zip(tiles, blocks):
        for s in range(tiles_ref.shape[0]):
            add_products(grid_ref, acc_refs, tiles_ref.at[s], blocks_ref.at[s])


def more_kernel(starts, *refs):
    n_sets = len(starts)
    grid_ref = refs[0]
    tiles, blocks = refs[3 : 3 + n_sets], refs[3 + n_sets : 3 + 2 * n_sets]
    acc_refs = refs[3 + 2 * n_sets :]
    for tiles_ref, blocks_ref, start in zip(tiles, blocks, starts):
        for s in range(tiles_ref.shape[0]):
            first = tiles_ref.shape[1] % TILE
            add_products(grid_ref, acc_refs, tiles_ref.at[s], blocks_ref.at[s], first, start)


def fold_kernel(shifts, own_ref, mirror_ref, keep_ref, send_ref):
    half = keep_ref.shape[1]
    core = lax.axis_index("pair") % 2
    vir = lax.axis_index("vir")
    swap = swap_matrix().astype(BF16)
    for place, shift in enumerate(shifts):
        for k in range(half):
            for out_ref, side in ((keep_ref, core), (send_ref, 1 - core)):
                block = ((vir ^ shift) * 2 + side) * half + k
                upper = mirror_ref[block].astype(BF16)
                total = own_ref[block] + jnp.dot(upper, swap, preferred_element_type=F32)
                out_ref[place, k] = total.astype(BF16)


def join_kernel(keep_ref, come_ref, *outs):
    for shift, out_ref in enumerate(outs):
        out_ref[...] = (keep_ref[shift].astype(F32) + come_ref[shift].astype(F32)).astype(BF16)


def total_kernel(*refs):
    total = refs[0][...].astype(F32)
    for ref in refs[1:-1]:
        total += ref[...].astype(F32)
    refs[-1][...] = total.astype(BF16)


def finish_kernel(own_ref, other_ref, hot_ref, out_ref, made_ref, sems):
    half = own_ref.shape[0]
    upper = lax.axis_index("pair") % 2 == 1
    hot = hot_ref[...]
    same = (iota((TILE, TILE), 0) == iota((TILE, TILE), 1)).astype(F32)
    swap = jnp.where(upper, swap_matrix().astype(F32), same).astype(BF16)
    copies = []
    for which in range(2):
        for k in range(half):
            values = jnp.where(upper == (which == 1), own_ref[k], other_ref[k])
            values = jnp.dot(values, swap, preferred_element_type=F32).astype(BF16)
            block = which * half + k
            columns = pl.ds(block * TILE, TILE)
            made_ref[:, columns] = jnp.dot(hot, values, preferred_element_type=F32).astype(BF16)
            copies.append(pltpu.make_async_copy(made_ref.at[:, columns], out_ref.at[:, columns], sems.at[block]))
            copies[-1].start()
    for copy in copies:
        copy.wait()


def local(amplitudes, integrals, tile_blocks, mirror_row):
    rows, width = amplitudes.shape
    slabs, tile_dev = integrals.shape[:2]
    n_pair, n_vir = lax.axis_size("pair"), lax.axis_size("vir")
    chips = n_pair // 2
    per = width // TILE
    n_blk = per * n_vir
    length = tile_dev * TILE

    def across(array, bits):
        return lax.ppermute(array, "pair", [(i, i ^ bits) for i in range(n_pair)])

    def along(array, bits):
        return lax.ppermute(array, "vir", [(i, i ^ bits) for i in range(n_vir)])

    ids = tile_blocks.transpose(0, 2, 1).reshape(1, 2 * slabs, tile_dev).astype(BF16)
    ids = jnp.pad(ids, ((0, 0), (0, EXTRA - 2 * slabs), (0, TILE - tile_dev)))
    ids = jnp.broadcast_to(ids, (slabs, EXTRA, TILE))
    packed = jnp.concatenate([ids, integrals.reshape(slabs, length, TILE)], axis=1)
    early = [packed, across(packed, 2), across(packed, 4)]

    pieces = {0: amplitudes}
    reach = n_vir // 2
    while reach:
        pieces |= {shift + reach: along(piece, reach) for shift, piece in pieces.items()}
        reach //= 2
    mine = [pieces[shift] for shift in range(n_vir)]
    others = [across(piece, 1) for piece in mine]
    first = [*others, *mine[1:]]
    middle = EXTRA + length // 2
    halves = call(
        functools.partial(cut_kernel, slabs),
        [jax.ShapeDtypeStruct((size, TILE), BF16) for _ in range(slabs) for size in (middle, length // 2)],
        [VMEM, VMEM] + [pl.BlockSpec(memory_space=pl.ANY)] * len(first),
        megabytes=4,
    )(early[1], early[2], *first)
    late = [[across(half, 4 if s % 2 == 0 else 2) for s, half in enumerate(halves[part::2])] for part in range(2)]
    farther, reach = [], 4
    while reach < chips:
        if reach == 4:
            diagonal = jnp.stack([jnp.concatenate([late[part][s] for part in range(2)]) for s in range(slabs)])
            farther = [across(array, 2 * reach) for array in (*early, diagonal)]
        else:
            farther += [across(array, 2 * reach) for array in (*early, diagonal, *farther)]
        reach *= 2
    row = mirror_row.reshape(1, rows)

    def ids_in(array):
        return array[: 2 * slabs, :tile_dev].astype(jnp.int32).reshape(slabs, 2, tile_dev)

    sums = jax.ShapeDtypeStruct((n_blk, rows, TILE), F32)
    grid, last_hot, *sums_so_far = call(
        functools.partial(first_kernel, n_vir, len(early)),
        [
            jax.ShapeDtypeStruct((n_blk, 2 * rows, TILE), BF16),
            jax.ShapeDtypeStruct((rows, rows), BF16),
            sums,
            sums,
        ],
        [VMEM] * (2 * n_vir + len(early)) + [SMEM] * len(early) + [VMEM],
        megabytes=20,
    )(*mine, *others, *early, tile_blocks.transpose(0, 2, 1), *[ids_in(array[0]) for array in early[1:]], row)
    diagonal_ids = ids_in(late[0][0])
    for part in range(2):
        more = [half[None] for half in late[part]] + (farther if part else [])
        more_ids = [diagonal_ids[s : s + 1] for s in range(slabs)]
        more_ids += [ids_in(array[0]) for array in farther] if part else []
        starts = [part * tile_dev // 2] * slabs + [0] * (len(more) - slabs)
        sums_so_far = call(
            functools.partial(more_kernel, starts),
            [sums, sums],
            [VMEM] * (3 + len(more)) + [SMEM] * len(more),
            megabytes=24,
            aliases={1: 0, 2: 1},
        )(grid, *sums_so_far, *more, *more_ids)

    parts = {}
    for shifts in (range(n_vir - 1, n_vir // 2 - 1, -1), range(n_vir // 2 - 1, -1, -1)):
        piece = jax.ShapeDtypeStruct((len(shifts), per // 2, rows, TILE), BF16)
        keep, send = call(
            functools.partial(fold_kernel, shifts), [piece, piece], [VMEM, VMEM], megabytes=8
        )(*sums_so_far)
        one = jax.ShapeDtypeStruct((per // 2, rows, TILE), BF16)
        joined = call(join_kernel, [one] * len(shifts), [VMEM, VMEM], megabytes=4)(keep, across(send, 1))
        parts |= {shift: along(part, shift) if shift else part for shift, part in zip(shifts, joined)}
    total = call(total_kernel, one, [VMEM] * n_vir, megabytes=4)(*[parts[shift] for shift in range(n_vir)])
    return call(
        finish_kernel,
        jax.ShapeDtypeStruct((rows, width), BF16),
        [VMEM] * 3,
        [pltpu.VMEM((rows, width), BF16), pltpu.SemaphoreType.DMA((per,))],
        megabytes=8,
        out_specs=pl.BlockSpec(memory_space=pl.ANY),
    )(total, across(total, 1), last_hot)


def solution(mesh):
    in_specs = (
        P("pair", "vir"),
        P(None, ("pair", "vir"), None, None),
        P(None, ("pair", "vir"), None),
        P("pair"),
    )
    out_specs = P("pair", "vir")
    return jax.shard_map(local, mesh=mesh, in_specs=in_specs, out_specs=out_specs, check_vma=False)
```

```python
import functools

import jax
import jax.numpy as jnp
from jax import lax
from jax.experimental import pallas as pl
from jax.experimental.pallas import tpu as pltpu
from jax.sharding import PartitionSpec as P

TILE = 128
SUB = 8
F32 = jnp.float32
BF16 = jnp.bfloat16
VMEM = pl.BlockSpec(memory_space=pltpu.VMEM)
SMEM = pl.BlockSpec(memory_space=pltpu.SMEM)


def call(body, out_shape, in_specs, scratch=(), megabytes=32, aliases=None, out_specs=None):
    many = isinstance(out_shape, (list, tuple))
    return pl.pallas_call(
        body,
        out_shape=out_shape,
        in_specs=in_specs,
        out_specs=out_specs or ([VMEM] * len(out_shape) if many else VMEM),
        scratch_shapes=list(scratch),
        compiler_params=pltpu.CompilerParams(vmem_limit_bytes=megabytes << 20),
        input_output_aliases=aliases or {},
        cost_estimate=pl.CostEstimate(flops=0, bytes_accessed=0, transcendentals=0),
    )


def iota(shape, dimension):
    return lax.broadcasted_iota(jnp.int32, shape, dimension)


def swap_matrix():
    target = iota((TILE, TILE), 1)
    h, a, b = target // (SUB * SUB), target // SUB % SUB, target % SUB
    return iota((TILE, TILE), 0) == (1 - h) * SUB * SUB + b * SUB + a


def copy_kernel(in_ref, *refs):
    refs[-1][...] = in_ref[...]


def cut_kernel(slabs, x_ref, y_ref, *refs):
    for s in range(slabs):
        slab_ref = (x_ref if s % 2 == 0 else y_ref).at[s]
        upper_ref, lower_ref = refs[2 * (s - slabs)], refs[2 * (s - slabs) + 1]
        middle = upper_ref.shape[0]
        upper_ref[...] = slab_ref[:middle]
        lower_ref[...] = slab_ref[middle:]


def add_products(grid_ref, acc_refs, tiles_ref, blocks_ref, start=0):
    empty = jnp.zeros((TILE, TILE), BF16)
    rows = acc_refs[0].shape[1]

    @pl.loop(0, tiles_ref.shape[0] // TILE // 2, unroll=4)
    def _(t):
        to, come = [[blocks_ref[which, start + 2 * t + k] for k in range(2)] for which in range(2)]
        tiles = [tiles_ref[pl.ds(pl.multiple_of((2 * t + k) * TILE, TILE), TILE), :] for k in range(2)]
        right = jnp.concatenate(
            [jnp.concatenate([tiles[0], empty], axis=1), jnp.concatenate([empty, tiles[1]], axis=1)], axis=0
        )
        products = []
        for side in range(2):
            part = slice(side * rows, (side + 1) * rows)
            left = jnp.concatenate([grid_ref[come[0], part], grid_ref[come[1], part]], axis=1)
            products.append(jnp.dot(left, right, preferred_element_type=F32))
        for k in range(2):
            for side in range(2):
                acc_refs[side][to[k]] += products[side][:, k * TILE : (k + 1) * TILE]


def first_kernel(n_vir, n_sets, *refs):
    own, other = refs[:n_vir], refs[n_vir : 2 * n_vir]
    tiles = refs[2 * n_vir : 2 * n_vir + n_sets]
    blocks = refs[2 * n_vir + n_sets : 2 * n_vir + 2 * n_sets]
    row_ref, grid_ref, last_hot_ref, *acc_refs = refs[2 * n_vir + 2 * n_sets :]
    rows, width = own[0].shape
    per = width // TILE
    pair = lax.axis_index("pair")
    vir = lax.axis_index("vir")
    upper = pair % 2 == 1
    mirrors = (row_ref[...] - (pair ^ 1) * rows == iota((rows, rows), 0)).astype(F32)
    turned = mirrors.T
    hot = jnp.where(upper, mirrors, turned).astype(BF16)
    same = (iota((rows, rows), 0) == iota((rows, rows), 1)).astype(F32)
    last_hot_ref[...] = jnp.where(upper, turned, same).astype(BF16)
    for shift in range(n_vir):
        first = (vir ^ shift) * per
        mine, others = own[shift][...], other[shift][...]
        kept = jnp.where(upper, others, mine)
        moved = jnp.dot(hot, jnp.where(upper, mine, others), preferred_element_type=F32).astype(BF16)
        for k in range(per):
            columns = slice(k * TILE, (k + 1) * TILE)
            grid_ref[first + k, :rows] = kept[:, columns]
            grid_ref[first + k, rows:] = moved[:, columns]
    for acc_ref in acc_refs:
        acc_ref[...] = jnp.zeros_like(acc_ref)
    for tiles_ref, blocks_ref in zip(tiles, blocks):
        for s in range(tiles_ref.shape[0]):
            add_products(grid_ref, acc_refs, tiles_ref.at[s], blocks_ref.at[s])


def more_kernel(starts, *refs):
    n_sets = len(starts)
    grid_ref = refs[0]
    tiles, blocks = refs[3 : 3 + n_sets], refs[3 + n_sets : 3 + 2 * n_sets]
    acc_refs = refs[3 + 2 * n_sets :]
    for tiles_ref, blocks_ref, start in zip(tiles, blocks, starts):
        for s in range(tiles_ref.shape[0]):
            add_products(grid_ref, acc_refs, tiles_ref.at[s], blocks_ref.at[s], start)


def fold_kernel(shifts, own_ref, mirror_ref, keep_ref, send_ref):
    half = keep_ref.shape[1]
    core = lax.axis_index("pair") % 2
    vir = lax.axis_index("vir")
    swap = swap_matrix().astype(BF16)
    for place, shift in enumerate(shifts):
        for k in range(half):
            for out_ref, side in ((keep_ref, core), (send_ref, 1 - core)):
                block = ((vir ^ shift) * 2 + side) * half + k
                upper = mirror_ref[block].astype(BF16)
                total = own_ref[block] + jnp.dot(upper, swap, preferred_element_type=F32)
                out_ref[place, k] = total.astype(BF16)


def join_kernel(keep_ref, come_ref, *outs):
    for shift, out_ref in enumerate(outs):
        out_ref[...] = (keep_ref[shift].astype(F32) + come_ref[shift].astype(F32)).astype(BF16)


def total_kernel(*refs):
    total = refs[0][...].astype(F32)
    for ref in refs[1:-1]:
        total += ref[...].astype(F32)
    refs[-1][...] = total.astype(BF16)


def finish_kernel(own_ref, other_ref, hot_ref, out_ref, made_ref, sems):
    half = own_ref.shape[0]
    upper = lax.axis_index("pair") % 2 == 1
    hot = hot_ref[...]
    same = (iota((TILE, TILE), 0) == iota((TILE, TILE), 1)).astype(F32)
    swap = jnp.where(upper, swap_matrix().astype(F32), same).astype(BF16)
    copies = []
    for which in range(2):
        for k in range(half):
            values = jnp.where(upper == (which == 1), own_ref[k], other_ref[k])
            values = jnp.dot(values, swap, preferred_element_type=F32).astype(BF16)
            block = which * half + k
            columns = pl.ds(block * TILE, TILE)
            made_ref[:, columns] = jnp.dot(hot, values, preferred_element_type=F32).astype(BF16)
            copies.append(pltpu.make_async_copy(made_ref.at[:, columns], out_ref.at[:, columns], sems.at[block]))
            copies[-1].start()
    for copy in copies:
        copy.wait()


def local(amplitudes, integrals, tile_blocks, mirror_row):
    rows, width = amplitudes.shape
    slabs, tile_dev = integrals.shape[:2]
    n_pair, n_vir = lax.axis_size("pair"), lax.axis_size("vir")
    chips = n_pair // 2
    per = width // TILE
    n_blk = per * n_vir
    length = tile_dev * TILE

    def across(array, bits):
        return lax.ppermute(array, "pair", [(i, i ^ bits) for i in range(n_pair)])

    def along(array, bits):
        return lax.ppermute(array, "vir", [(i, i ^ bits) for i in range(n_vir)])

    tiles = integrals.reshape(slabs, length, TILE)
    early = [tiles, across(tiles, 2), across(tiles, 4)]

    pieces = {0: amplitudes}
    reach = n_vir // 2
    while reach:
        pieces |= {shift + reach: along(piece, reach) for shift, piece in pieces.items()}
        reach //= 2
    mine = [pieces[shift] for shift in range(n_vir)]
    others = [across(piece, 1) for piece in mine]
    ids = tile_blocks.transpose(0, 2, 1)
    anywhere = pl.BlockSpec(memory_space=pl.ANY)
    first = [others[n_vir // 2], others[1]]
    held = call(
        copy_kernel, jax.ShapeDtypeStruct(ids.shape, ids.dtype), [VMEM, anywhere, anywhere], megabytes=4
    )(ids, *first)
    blocks = [ids] + [across(held, 2 * d) for d in range(1, chips)]
    first = [*others, *mine[1:], *blocks[1:]]
    halves = call(
        functools.partial(cut_kernel, slabs),
        [jax.ShapeDtypeStruct((length // 2, TILE), BF16)] * (2 * slabs),
        [VMEM, VMEM] + [anywhere] * len(first),
        megabytes=4,
    )(early[1], early[2], *first)
    late = [[across(half, 4 if s % 2 == 0 else 2) for s, half in enumerate(halves[part::2])] for part in range(2)]
    farther, reach = [], 4
    while reach < chips:
        if reach == 4:
            diagonal = jnp.stack([jnp.concatenate([late[part][s] for part in range(2)]) for s in range(slabs)])
            farther = [across(array, 2 * reach) for array in (*early, diagonal)]
        else:
            farther += [across(array, 2 * reach) for array in (*early, diagonal, *farther)]
        reach *= 2
    row = mirror_row.reshape(1, rows)

    sums = jax.ShapeDtypeStruct((n_blk, rows, TILE), F32)
    grid, last_hot, *sums_so_far = call(
        functools.partial(first_kernel, n_vir, len(early)),
        [
            jax.ShapeDtypeStruct((n_blk, 2 * rows, TILE), BF16),
            jax.ShapeDtypeStruct((rows, rows), BF16),
            sums,
            sums,
        ],
        [VMEM] * (2 * n_vir + len(early)) + [SMEM] * len(early) + [VMEM],
        megabytes=20,
    )(*mine, *others, *early, *blocks[:3], row)
    for part in range(2):
        more = [half[None] for half in late[part]] + (farther if part else [])
        more_ids = [blocks[3][s : s + 1] for s in range(slabs)] + (blocks[4:] if part else [])
        starts = [part * tile_dev // 2] * slabs + [0] * (len(more) - slabs)
        sums_so_far = call(
            functools.partial(more_kernel, starts),
            [sums, sums],
            [VMEM] * (3 + len(more)) + [SMEM] * len(more),
            megabytes=24,
            aliases={1: 0, 2: 1},
        )(grid, *sums_so_far, *more, *more_ids)

    parts = {}
    for shifts in (range(n_vir - 1, n_vir // 2 - 1, -1), range(n_vir // 2 - 1, -1, -1)):
        piece = jax.ShapeDtypeStruct((len(shifts), per // 2, rows, TILE), BF16)
        keep, send = call(
            functools.partial(fold_kernel, shifts), [piece, piece], [VMEM, VMEM], megabytes=8
        )(*sums_so_far)
        one = jax.ShapeDtypeStruct((per // 2, rows, TILE), BF16)
        joined = call(join_kernel, [one] * len(shifts), [VMEM, VMEM], megabytes=4)(keep, across(send, 1))
        parts |= {shift: along(part, shift) if shift else part for shift, part in zip(shifts, joined)}
    total = call(total_kernel, one, [VMEM] * n_vir, megabytes=4)(*[parts[shift] for shift in range(n_vir)])
    return call(
        finish_kernel,
        jax.ShapeDtypeStruct((rows, width), BF16),
        [VMEM] * 3,
        [pltpu.VMEM((rows, width), BF16), pltpu.SemaphoreType.DMA((per,))],
        megabytes=8,
        out_specs=pl.BlockSpec(memory_space=pl.ANY),
    )(total, across(total, 1), last_hot)


def solution(mesh):
    in_specs = (
        P("pair", "vir"),
        P(None, ("pair", "vir"), None, None),
        P(None, ("pair", "vir"), None),
        P("pair"),
    )
    out_specs = P("pair", "vir")
    return jax.shard_map(local, mesh=mesh, in_specs=in_specs, out_specs=out_specs, check_vma=False)
```

```python
import functools

import jax
import jax.numpy as jnp
from jax import lax
from jax.experimental import pallas as pl
from jax.experimental.pallas import tpu as pltpu
from jax.sharding import PartitionSpec as P

TILE = 128
SUB = 8
F32 = jnp.float32
BF16 = jnp.bfloat16
VMEM = pl.BlockSpec(memory_space=pltpu.VMEM)
SMEM = pl.BlockSpec(memory_space=pltpu.SMEM)


def call(body, out_shape, in_specs, scratch=(), megabytes=32, aliases=None, out_specs=None):
    many = isinstance(out_shape, (list, tuple))
    return pl.pallas_call(
        body,
        out_shape=out_shape,
        in_specs=in_specs,
        out_specs=out_specs or ([VMEM] * len(out_shape) if many else VMEM),
        scratch_shapes=list(scratch),
        compiler_params=pltpu.CompilerParams(vmem_limit_bytes=megabytes << 20),
        input_output_aliases=aliases or {},
        cost_estimate=pl.CostEstimate(flops=0, bytes_accessed=0, transcendentals=0),
    )


def iota(shape, dimension):
    return lax.broadcasted_iota(jnp.int32, shape, dimension)


def swap_matrix():
    target = iota((TILE, TILE), 1)
    h, a, b = target // (SUB * SUB), target // SUB % SUB, target % SUB
    return iota((TILE, TILE), 0) == (1 - h) * SUB * SUB + b * SUB + a


def copy_kernel(in_ref, *refs):
    refs[-1][...] = in_ref[...]


def cut_kernel(slabs, x_ref, y_ref, *refs):
    for s in range(slabs):
        slab_ref = (x_ref if s % 2 == 0 else y_ref).at[s]
        upper_ref, lower_ref = refs[2 * (s - slabs)], refs[2 * (s - slabs) + 1]
        middle = upper_ref.shape[0]
        upper_ref[...] = slab_ref[:middle]
        lower_ref[...] = slab_ref[middle:]


def add_products(grid_ref, acc_refs, tiles_ref, blocks_ref, start=0):
    empty = jnp.zeros((TILE, TILE), BF16)
    rows = acc_refs[0].shape[1]

    @pl.loop(0, tiles_ref.shape[0] // TILE // 2, unroll=4)
    def _(t):
        to, come = [[blocks_ref[which, start + 2 * t + k] for k in range(2)] for which in range(2)]
        tiles = [tiles_ref[pl.ds(pl.multiple_of((2 * t + k) * TILE, TILE), TILE), :] for k in range(2)]
        right = jnp.concatenate(
            [jnp.concatenate([tiles[0], empty], axis=1), jnp.concatenate([empty, tiles[1]], axis=1)], axis=0
        )
        products = []
        for side in range(2):
            part = slice(side * rows, (side + 1) * rows)
            left = jnp.concatenate([grid_ref[come[0], part], grid_ref[come[1], part]], axis=1)
            products.append(jnp.dot(left, right, preferred_element_type=F32))
        for k in range(2):
            for side in range(2):
                acc_refs[side][to[k]] += products[side][:, k * TILE : (k + 1) * TILE]


def first_kernel(n_vir, n_sets, *refs):
    own, other = refs[:n_vir], refs[n_vir : 2 * n_vir]
    tiles = refs[2 * n_vir : 2 * n_vir + n_sets]
    blocks = refs[2 * n_vir + n_sets : 2 * n_vir + 2 * n_sets]
    row_ref, grid_ref, last_hot_ref, *acc_refs = refs[2 * n_vir + 2 * n_sets :]
    rows, width = own[0].shape
    per = width // TILE
    pair = lax.axis_index("pair")
    vir = lax.axis_index("vir")
    upper = pair % 2 == 1
    mirrors = (row_ref[...] - (pair ^ 1) * rows == iota((rows, rows), 0)).astype(F32)
    turned = mirrors.T
    hot = jnp.where(upper, mirrors, turned).astype(BF16)
    same = (iota((rows, rows), 0) == iota((rows, rows), 1)).astype(F32)
    last_hot_ref[...] = jnp.where(upper, turned, same).astype(BF16)
    for shift in range(n_vir):
        first = (vir ^ shift) * per
        mine, others = own[shift][...], other[shift][...]
        kept = jnp.where(upper, others, mine)
        moved = jnp.dot(hot, jnp.where(upper, mine, others), preferred_element_type=F32).astype(BF16)
        for k in range(per):
            columns = slice(k * TILE, (k + 1) * TILE)
            grid_ref[first + k, :rows] = kept[:, columns]
            grid_ref[first + k, rows:] = moved[:, columns]
    for acc_ref in acc_refs:
        acc_ref[...] = jnp.zeros_like(acc_ref)
    for tiles_ref, blocks_ref in zip(tiles, blocks):
        for s in range(tiles_ref.shape[0]):
            add_products(grid_ref, acc_refs, tiles_ref.at[s], blocks_ref.at[s])


def more_kernel(starts, *refs):
    n_sets = len(starts)
    grid_ref = refs[0]
    tiles, blocks = refs[3 : 3 + n_sets], refs[3 + n_sets : 3 + 2 * n_sets]
    acc_refs = refs[3 + 2 * n_sets :]
    for tiles_ref, blocks_ref, start in zip(tiles, blocks, starts):
        for s in range(tiles_ref.shape[0]):
            add_products(grid_ref, acc_refs, tiles_ref.at[s], blocks_ref.at[s], start)


def fold_kernel(shifts, own_ref, mirror_ref, keep_ref, send_ref):
    half = keep_ref.shape[1]
    core = lax.axis_index("pair") % 2
    vir = lax.axis_index("vir")
    swap = swap_matrix().astype(BF16)
    for place, shift in enumerate(shifts):
        for k in range(half):
            for out_ref, side in ((keep_ref, core), (send_ref, 1 - core)):
                block = ((vir ^ shift) * 2 + side) * half + k
                upper = mirror_ref[block].astype(BF16)
                total = own_ref[block] + jnp.dot(upper, swap, preferred_element_type=F32)
                out_ref[place, k] = total.astype(BF16)


def join_kernel(keep_ref, come_ref, *outs):
    for shift, out_ref in enumerate(outs):
        out_ref[...] = (keep_ref[shift].astype(F32) + come_ref[shift].astype(F32)).astype(BF16)


def total_kernel(*refs):
    total = refs[0][...].astype(F32)
    for ref in refs[1:-1]:
        total += ref[...].astype(F32)
    refs[-1][...] = total.astype(BF16)


def finish_kernel(own_ref, other_ref, hot_ref, out_ref, made_ref, sems):
    half = own_ref.shape[0]
    upper = lax.axis_index("pair") % 2 == 1
    hot = hot_ref[...]
    same = (iota((TILE, TILE), 0) == iota((TILE, TILE), 1)).astype(F32)
    swap = jnp.where(upper, swap_matrix().astype(F32), same).astype(BF16)
    copies = []
    for which in range(2):
        for k in range(half):
            values = jnp.where(upper == (which == 1), own_ref[k], other_ref[k])
            values = jnp.dot(values, swap, preferred_element_type=F32).astype(BF16)
            block = which * half + k
            columns = pl.ds(block * TILE, TILE)
            made_ref[:, columns] = jnp.dot(hot, values, preferred_element_type=F32).astype(BF16)
            copies.append(pltpu.make_async_copy(made_ref.at[:, columns], out_ref.at[:, columns], sems.at[block]))
            copies[-1].start()
    for copy in copies:
        copy.wait()


def local(amplitudes, integrals, tile_blocks, mirror_row):
    rows, width = amplitudes.shape
    slabs, tile_dev = integrals.shape[:2]
    n_pair, n_vir = lax.axis_size("pair"), lax.axis_size("vir")
    chips = n_pair // 2
    per = width // TILE
    n_blk = per * n_vir
    length = tile_dev * TILE

    def across(array, bits):
        return lax.ppermute(array, "pair", [(i, i ^ bits) for i in range(n_pair)])

    def along(array, bits):
        return lax.ppermute(array, "vir", [(i, i ^ bits) for i in range(n_vir)])

    tiles = integrals.reshape(slabs, length, TILE)
    early = [tiles, across(tiles, 2), across(tiles, 4)]

    pieces = {0: amplitudes}
    reach = n_vir // 2
    while reach:
        pieces |= {shift + reach: along(piece, reach) for shift, piece in pieces.items()}
        reach //= 2
    mine = [pieces[shift] for shift in range(n_vir)]
    others = [across(piece, 1) for piece in mine]
    ids = tile_blocks.transpose(0, 2, 1)
    anywhere = pl.BlockSpec(memory_space=pl.ANY)
    first = [pieces[n_vir // 2]]
    held = call(
        copy_kernel, jax.ShapeDtypeStruct(ids.shape, ids.dtype), [VMEM, anywhere], megabytes=4
    )(ids, *first)
    blocks = [ids] + [across(held, 2 * d) for d in range(1, chips)]
    first = [*others, *mine[1:], *blocks[1:]]
    halves = call(
        functools.partial(cut_kernel, slabs),
        [jax.ShapeDtypeStruct((length // 2, TILE), BF16)] * (2 * slabs),
        [VMEM, VMEM] + [anywhere] * len(first),
        megabytes=4,
    )(early[1], early[2], *first)
    late = [[across(half, 4 if s % 2 == 0 else 2) for s, half in enumerate(halves[part::2])] for part in range(2)]
    farther, reach = [], 4
    while reach < chips:
        if reach == 4:
            diagonal = jnp.stack([jnp.concatenate([late[part][s] for part in range(2)]) for s in range(slabs)])
            farther = [across(array, 2 * reach) for array in (*early, diagonal)]
        else:
            farther += [across(array, 2 * reach) for array in (*early, diagonal, *farther)]
        reach *= 2
    row = mirror_row.reshape(1, rows)

    sums = jax.ShapeDtypeStruct((n_blk, rows, TILE), F32)
    grid, last_hot, *sums_so_far = call(
        functools.partial(first_kernel, n_vir, len(early)),
        [
            jax.ShapeDtypeStruct((n_blk, 2 * rows, TILE), BF16),
            jax.ShapeDtypeStruct((rows, rows), BF16),
            sums,
            sums,
        ],
        [VMEM] * (2 * n_vir + len(early)) + [SMEM] * len(early) + [VMEM],
        megabytes=20,
    )(*mine, *others, *early, *blocks[:3], row)
    for part in range(2):
        more = [half[None] for half in late[part]] + (farther if part else [])
        more_ids = [blocks[3][s : s + 1] for s in range(slabs)] + (blocks[4:] if part else [])
        starts = [part * tile_dev // 2] * slabs + [0] * (len(more) - slabs)
        sums_so_far = call(
            functools.partial(more_kernel, starts),
            [sums, sums],
            [VMEM] * (3 + len(more)) + [SMEM] * len(more),
            megabytes=24,
            aliases={1: 0, 2: 1},
        )(grid, *sums_so_far, *more, *more_ids)

    parts = {}
    for shifts in (range(n_vir - 1, n_vir // 2 - 1, -1), range(n_vir // 2 - 1, -1, -1)):
        piece = jax.ShapeDtypeStruct((len(shifts), per // 2, rows, TILE), BF16)
        keep, send = call(
            functools.partial(fold_kernel, shifts), [piece, piece], [VMEM, VMEM], megabytes=8
        )(*sums_so_far)
        one = jax.ShapeDtypeStruct((per // 2, rows, TILE), BF16)
        joined = call(join_kernel, [one] * len(shifts), [VMEM, VMEM], megabytes=4)(keep, across(send, 1))
        parts |= {shift: along(part, shift) if shift else part for shift, part in zip(shifts, joined)}
    total = call(total_kernel, one, [VMEM] * n_vir, megabytes=4)(*[parts[shift] for shift in range(n_vir)])
    return call(
        finish_kernel,
        jax.ShapeDtypeStruct((rows, width), BF16),
        [VMEM] * 3,
        [pltpu.VMEM((rows, width), BF16), pltpu.SemaphoreType.DMA((per,))],
        megabytes=8,
        out_specs=pl.BlockSpec(memory_space=pl.ANY),
    )(total, across(total, 1), last_hot)


def solution(mesh):
    in_specs = (
        P("pair", "vir"),
        P(None, ("pair", "vir"), None, None),
        P(None, ("pair", "vir"), None),
        P("pair"),
    )
    out_specs = P("pair", "vir")
    return jax.shard_map(local, mesh=mesh, in_specs=in_specs, out_specs=out_specs, check_vma=False)
```

```python
import functools

import jax
import jax.numpy as jnp
from jax import lax
from jax.experimental import pallas as pl
from jax.experimental.pallas import tpu as pltpu
from jax.sharding import PartitionSpec as P

TILE = 128
SUB = 8
EXTRA = 16
F32 = jnp.float32
BF16 = jnp.bfloat16
VMEM = pl.BlockSpec(memory_space=pltpu.VMEM)
SMEM = pl.BlockSpec(memory_space=pltpu.SMEM)


def call(body, out_shape, in_specs, scratch=(), megabytes=32, aliases=None, out_specs=None):
    many = isinstance(out_shape, (list, tuple))
    return pl.pallas_call(
        body,
        out_shape=out_shape,
        in_specs=in_specs,
        out_specs=out_specs or ([VMEM] * len(out_shape) if many else VMEM),
        scratch_shapes=list(scratch),
        compiler_params=pltpu.CompilerParams(vmem_limit_bytes=megabytes << 20),
        input_output_aliases=aliases or {},
        cost_estimate=pl.CostEstimate(flops=0, bytes_accessed=0, transcendentals=0),
    )


def iota(shape, dimension):
    return lax.broadcasted_iota(jnp.int32, shape, dimension)


def swap_matrix():
    target = iota((TILE, TILE), 1)
    h, a, b = target // (SUB * SUB), target // SUB % SUB, target % SUB
    return iota((TILE, TILE), 0) == (1 - h) * SUB * SUB + b * SUB + a


def cut_kernel(slabs, x_ref, y_ref, *refs):
    for s in range(slabs):
        slab_ref = (x_ref if s % 2 == 0 else y_ref).at[s]
        upper_ref, lower_ref = refs[2 * (s - slabs)], refs[2 * (s - slabs) + 1]
        middle = upper_ref.shape[0]
        upper_ref[...] = slab_ref[:middle]
        lower_ref[...] = slab_ref[middle:]


def add_products(grid_ref, acc_refs, tiles_ref, blocks_ref, first=EXTRA, start=0):
    empty = jnp.zeros((TILE, TILE), BF16)
    rows = acc_refs[0].shape[1]

    @pl.loop(0, tiles_ref.shape[0] // TILE // 2, unroll=4)
    def _(t):
        to, come = [[blocks_ref[which, start + 2 * t + k] for k in range(2)] for which in range(2)]
        tiles = [tiles_ref[pl.ds(pl.multiple_of((2 * t + k) * TILE + first, EXTRA), TILE), :] for k in range(2)]
        right = jnp.concatenate(
            [jnp.concatenate([tiles[0], empty], axis=1), jnp.concatenate([empty, tiles[1]], axis=1)], axis=0
        )
        products = []
        for side in range(2):
            part = slice(side * rows, (side + 1) * rows)
            left = jnp.concatenate([grid_ref[come[0], part], grid_ref[come[1], part]], axis=1)
            products.append(jnp.dot(left, right, preferred_element_type=F32))
        for k in range(2):
            for side in range(2):
                acc_refs[side][to[k]] += products[side][:, k * TILE : (k + 1) * TILE]


def first_kernel(n_vir, n_sets, *refs):
    own, other = refs[:n_vir], refs[n_vir : 2 * n_vir]
    tiles = refs[2 * n_vir : 2 * n_vir + n_sets]
    blocks = refs[2 * n_vir + n_sets : 2 * n_vir + 2 * n_sets]
    row_ref, grid_ref, last_hot_ref, *acc_refs = refs[2 * n_vir + 2 * n_sets :]
    rows, width = own[0].shape
    per = width // TILE
    pair = lax.axis_index("pair")
    vir = lax.axis_index("vir")
    upper = pair % 2 == 1
    mirrors = (row_ref[...] - (pair ^ 1) * rows == iota((rows, rows), 0)).astype(F32)
    turned = mirrors.T
    hot = jnp.where(upper, mirrors, turned).astype(BF16)
    same = (iota((rows, rows), 0) == iota((rows, rows), 1)).astype(F32)
    last_hot_ref[...] = jnp.where(upper, turned, same).astype(BF16)
    for shift in range(n_vir):
        first = (vir ^ shift) * per
        mine, others = own[shift][...], other[shift][...]
        kept = jnp.where(upper, others, mine)
        moved = jnp.dot(hot, jnp.where(upper, mine, others), preferred_element_type=F32).astype(BF16)
        for k in range(per):
            columns = slice(k * TILE, (k + 1) * TILE)
            grid_ref[first + k, :rows] = kept[:, columns]
            grid_ref[first + k, rows:] = moved[:, columns]
    for acc_ref in acc_refs:
        acc_ref[...] = jnp.zeros_like(acc_ref)
    for tiles_ref, blocks_ref in zip(tiles, blocks):
        for s in range(tiles_ref.shape[0]):
            add_products(grid_ref, acc_refs, tiles_ref.at[s], blocks_ref.at[s])


def more_kernel(starts, *refs):
    n_sets = len(starts)
    grid_ref = refs[0]
    tiles, blocks = refs[3 : 3 + n_sets], refs[3 + n_sets : 3 + 2 * n_sets]
    acc_refs = refs[3 + 2 * n_sets :]
    for tiles_ref, blocks_ref, start in zip(tiles, blocks, starts):
        for s in range(tiles_ref.shape[0]):
            first = tiles_ref.shape[1] % TILE
            add_products(grid_ref, acc_refs, tiles_ref.at[s], blocks_ref.at[s], first, start)


def fold_kernel(shifts, own_ref, mirror_ref, keep_ref, send_ref):
    half = keep_ref.shape[1]
    core = lax.axis_index("pair") % 2
    vir = lax.axis_index("vir")
    swap = swap_matrix().astype(BF16)
    for place, shift in enumerate(shifts):
        for k in range(half):
            for out_ref, side in ((keep_ref, core), (send_ref, 1 - core)):
                block = ((vir ^ shift) * 2 + side) * half + k
                upper = mirror_ref[block].astype(BF16)
                total = own_ref[block] + jnp.dot(upper, swap, preferred_element_type=F32)
                out_ref[place, k] = total.astype(BF16)


def join_kernel(keep_ref, come_ref, *outs):
    for shift, out_ref in enumerate(outs):
        out_ref[...] = (keep_ref[shift].astype(F32) + come_ref[shift].astype(F32)).astype(BF16)


def total_kernel(*refs):
    total = refs[0][...].astype(F32)
    for ref in refs[1:-1]:
        total += ref[...].astype(F32)
    refs[-1][...] = total.astype(BF16)


def order_half(hot, half_ref, place):
    upper = lax.axis_index("pair") % 2 == 1
    same = (iota((TILE, TILE), 0) == iota((TILE, TILE), 1)).astype(F32)
    swap = jnp.where(upper, swap_matrix().astype(F32), same).astype(BF16)
    for k in range(half_ref.shape[0]):
        values = jnp.dot(half_ref[k], swap, preferred_element_type=F32).astype(BF16)
        place(k, jnp.dot(hot, values, preferred_element_type=F32).astype(BF16))


def own_half_kernel(half_ref, hot_ref, out_ref):
    def place(k, values):
        out_ref[k] = values

    order_half(hot_ref[...], half_ref, place)


def finish_kernel(ordered_ref, other_ref, hot_ref, out_ref):
    half = other_ref.shape[0]
    upper = lax.axis_index("pair") % 2 == 1

    def place(k, values):
        ordered = ordered_ref[k]
        low, high = slice(k * TILE, (k + 1) * TILE), slice((half + k) * TILE, (half + k + 1) * TILE)
        out_ref[:, low] = jnp.where(upper, values, ordered)
        out_ref[:, high] = jnp.where(upper, ordered, values)

    order_half(hot_ref[...], other_ref, place)


def local(amplitudes, integrals, tile_blocks, mirror_row):
    rows, width = amplitudes.shape
    slabs, tile_dev = integrals.shape[:2]
    n_pair, n_vir = lax.axis_size("pair"), lax.axis_size("vir")
    chips = n_pair // 2
    per = width // TILE
    n_blk = per * n_vir
    length = tile_dev * TILE

    def across(array, bits):
        return lax.ppermute(array, "pair", [(i, i ^ bits) for i in range(n_pair)])

    def along(array, bits):
        return lax.ppermute(array, "vir", [(i, i ^ bits) for i in range(n_vir)])

    ids = tile_blocks.transpose(0, 2, 1).reshape(1, 2 * slabs, tile_dev).astype(BF16)
    ids = jnp.pad(ids, ((0, 0), (0, EXTRA - 2 * slabs), (0, TILE - tile_dev)))
    ids = jnp.broadcast_to(ids, (slabs, EXTRA, TILE))
    packed = jnp.concatenate([ids, integrals.reshape(slabs, length, TILE)], axis=1)
    early = [packed, across(packed, 2), across(packed, 4)]

    pieces = {0: amplitudes}
    reach = n_vir // 2
    while reach:
        pieces |= {shift + reach: along(piece, reach) for shift, piece in pieces.items()}
        reach //= 2
    mine = [pieces[shift] for shift in range(n_vir)]
    others = [across(piece, 1) for piece in mine]
    first = [*others, *mine[1:]]
    middle = EXTRA + length // 2
    halves = call(
        functools.partial(cut_kernel, slabs),
        [jax.ShapeDtypeStruct((size, TILE), BF16) for _ in range(slabs) for size in (middle, length // 2)],
        [VMEM, VMEM] + [pl.BlockSpec(memory_space=pl.ANY)] * len(first),
        megabytes=4,
    )(early[1], early[2], *first)
    late = [[across(half, 4 if s % 2 == 0 else 2) for s, half in enumerate(halves[part::2])] for part in range(2)]
    farther, reach = [], 4
    while reach < chips:
        if reach == 4:
            diagonal = jnp.stack([jnp.concatenate([late[part][s] for part in range(2)]) for s in range(slabs)])
            farther = [across(array, 2 * reach) for array in (*early, diagonal)]
        else:
            farther += [across(array, 2 * reach) for array in (*early, diagonal, *farther)]
        reach *= 2
    row = mirror_row.reshape(1, rows)

    def ids_in(array):
        return array[: 2 * slabs, :tile_dev].astype(jnp.int32).reshape(slabs, 2, tile_dev)

    sums = jax.ShapeDtypeStruct((n_blk, rows, TILE), F32)
    grid, last_hot, *sums_so_far = call(
        functools.partial(first_kernel, n_vir, len(early)),
        [
            jax.ShapeDtypeStruct((n_blk, 2 * rows, TILE), BF16),
            jax.ShapeDtypeStruct((rows, rows), BF16),
            sums,
            sums,
        ],
        [VMEM] * (2 * n_vir + len(early)) + [SMEM] * len(early) + [VMEM],
        megabytes=20,
    )(*mine, *others, *early, tile_blocks.transpose(0, 2, 1), *[ids_in(array[0]) for array in early[1:]], row)
    diagonal_ids = ids_in(late[0][0])
    for part in range(2):
        more = [half[None] for half in late[part]] + (farther if part else [])
        more_ids = [diagonal_ids[s : s + 1] for s in range(slabs)]
        more_ids += [ids_in(array[0]) for array in farther] if part else []
        starts = [part * tile_dev // 2] * slabs + [0] * (len(more) - slabs)
        sums_so_far = call(
            functools.partial(more_kernel, starts),
            [sums, sums],
            [VMEM] * (3 + len(more)) + [SMEM] * len(more),
            megabytes=24,
            aliases={1: 0, 2: 1},
        )(grid, *sums_so_far, *more, *more_ids)

    parts = {}
    for shifts in (range(n_vir - 1, n_vir // 2 - 1, -1), range(n_vir // 2 - 1, -1, -1)):
        piece = jax.ShapeDtypeStruct((len(shifts), per // 2, rows, TILE), BF16)
        keep, send = call(
            functools.partial(fold_kernel, shifts), [piece, piece], [VMEM, VMEM], megabytes=8
        )(*sums_so_far)
        one = jax.ShapeDtypeStruct((per // 2, rows, TILE), BF16)
        joined = call(join_kernel, [one] * len(shifts), [VMEM, VMEM], megabytes=4)(keep, across(send, 1))
        parts |= {shift: along(part, shift) if shift else part for shift, part in zip(shifts, joined)}
    total = call(total_kernel, one, [VMEM] * n_vir, megabytes=4)(*[parts[shift] for shift in range(n_vir)])
    ordered = call(own_half_kernel, one, [VMEM, VMEM], megabytes=4)(total, last_hot)
    return call(
        finish_kernel, jax.ShapeDtypeStruct((rows, width), BF16), [VMEM] * 3, megabytes=8
    )(ordered, across(total, 1), last_hot)


def solution(mesh):
    in_specs = (
        P("pair", "vir"),
        P(None, ("pair", "vir"), None, None),
        P(None, ("pair", "vir"), None),
        P("pair"),
    )
    out_specs = P("pair", "vir")
    return jax.shard_map(local, mesh=mesh, in_specs=in_specs, out_specs=out_specs, check_vma=False)
```
